512 devices in a mesh: tile: 16 (over x_hi, z), sect: 4 (over x_lo, core), emu: 8 (over y).
Axes of the slice: x: 4 (x_hi: 2, x_lo: 2; x = x_hi * 2 + x_lo), y: 8, z: 8, core: 2. Of those that a mesh axis runs over, the one named last changes fastest.
Arguments:
- state: float32 [8, 16, 256, 512], P(None, None, 'tile', ('sect', 'emu')), may hold values from -6 to 6
- winds: float32 [2, 16, 256, 512], P(None, None, 'tile', ('sect', 'emu')), may hold values from -0.5 to 0.5
- regime_table: int32 [16, 32, 256, 1], P('tile', ('sect', 'emu')), may hold values from 0 to 3; in each aligned block of 256 rows (0 to 255, 256 to 511, ..., all dimensions but the last counted through in order) at most 128 rows name the same one
- emu_lift: bfloat16 [4, 128, 8], P('sect'), may hold values from -2 to 2
- emu_conv: bfloat16 [4, 4, 3, 128, 128], P('sect'), may hold values from -0.3125 to 0.3125
- emu_output: bfloat16 [4, 8, 128], P('sect'), may hold values from -0.5 to 0.5
Outputs:
- final_state: float32 [8, 16, 256, 512], P(None, None, 'tile', ('sect', 'emu'))
The draws below stay inside these ranges and needn't reach their ends.
Inputs may be any that keep to these rules, and one draw needn't show every extreme that they name: `regime_table`: among the columns of one device (one block of the table), no regime is named more than 128 times, and in every draw some block names one regime exactly 128 times.
All inputs are finite; a program needn't handle non-finite values.
Results may differ from the reference program's by a relative error of at most 0.025.
Values may be sent and summed in bfloat16 or wider, within the bound.
A program may use at most 128 MiB of HBM per device.

```python
import math
import jax
import jax.numpy as jnp
import numpy as np
from jax import lax

VARS = 8
LEV = 16
CH = 128
LAYERS = 4
STEPS = 2
CX = 16
CY = 16
NX = 256
NY = 512
REG = 4
CAP = 128
N_TILE = 16
N_SECT = 4
N_EMU = 8


def block_levels(stream_key, dims, shards, low, largest):
    gain = 1.0
    for dim, shards_of in shards:
        draws = jax.random.uniform(jax.random.fold_in(jax.random.fold_in(stream_key, 6), dim), (shards_of,), jnp.float32, low / len(shards), largest / len(shards))
        gain = gain * jnp.repeat(jnp.exp(draws), dims[dim] // shards_of).reshape((-1,) + (1,) * (len(dims) - 1 - dim))
    return gain


def assign_block(key, own, number, rows, count, top, most, lean):
    ranking = jax.random.permutation(key, count)
    crowded, ordinary = shares(count, rows * top, most, lean, True), shares(count, rows * top, most, lean, False)
    places = jnp.arange(count)

    def named(lengths, rotation):
        used = int((lengths > 0).sum())
        fixed = max(1, used // 4)
        moved = fixed + (places - fixed + rotation * (used - fixed)) % max(1, count - fixed)
        return jnp.zeros((count,), jnp.int32).at[ranking[jnp.where(places < fixed, places, moved)]].set(jnp.asarray(lengths, jnp.int32))

    lengths = jnp.where(number % 4 == 0, named(crowded, number // 4), named(ordinary, number - number // 4 - 1))
    mixed = jax.random.permutation(jax.random.fold_in(own, 3), count)
    giver, taker = mixed[0:count // 2 * 2:2], mixed[1:count // 2 * 2:2]
    slack = jnp.minimum(lengths[giver] - 1, most - lengths[taker]) // 2
    slack = jnp.where((giver == ranking[0]) | (taker == ranking[0]) | (lengths[taker] == 0), 0, jnp.maximum(slack, 0))
    moved = jax.random.randint(jax.random.fold_in(own, 4), (count // 2,), 0, 1 << 20) % (slack + 1)
    lengths = lengths.at[giver].add(-moved).at[taker].add(moved)
    members = jnp.searchsorted(jnp.cumsum(lengths), jnp.arange(rows * top), side="right").astype(jnp.int32)
    listing = members.reshape(top, rows).T
    listing = listing[jax.random.permutation(jax.random.fold_in(own, 1), rows)]
    rotation = jax.random.randint(jax.random.fold_in(own, 2), (rows, 1), 0, top)
    return jnp.take_along_axis(listing, (jnp.arange(top)[None, :] + rotation) % top, axis=1)


def shares(amount, total, limit, skew, full):
    portions = [(1 << 20) // math.isqrt(standing ** skew) + 1 for standing in range(1, amount + 1)]
    largest = limit if full else min(limit, max(-(-total // amount), total * portions[0] // sum(portions)))
    least = 1 if total - largest >= amount - 1 else 0
    given, spare = [largest] + [least] * (amount - 1), total - largest - least * (amount - 1)
    while spare > 0:
        free = [i for i in range(1, amount) if given[i] < largest] or [i for i in range(1, amount) if given[i] < limit]
        pool, budget = sum([portions[i] for i in free]), spare
        for i in free:
            extra = min(limit - given[i], max(1, budget * portions[i] // pool), spare)
            given[i] = given[i] + extra
            spare = spare - extra
    return np.array(given)


def noise(own_key, shape, width, bound, cuts=(), kind=jnp.bfloat16):
    level = block_levels(own_key, shape, cuts, -0.22, 0.18) if cuts else 1.0
    entries = jax.random.normal(own_key, shape, jnp.float32) * width * level
    return jnp.minimum(jnp.maximum(entries, -bound), bound).astype(kind)


def setup_inputs(seed: int = 0) -> dict:
    splits = jax.random.split(jax.random.key(seed), 7)
    state = noise(splits[0], (VARS, LEV, NX, NY), 1.0, 6.0, ((2, 16), (3, 32)), jnp.float32)
    winds = jnp.clip(jax.random.uniform(splits[1], (2, LEV, NX, NY), jnp.float32, -0.5, 0.5) * block_levels(splits[1], (2, LEV, NX, NY), ((2, 16), (3, 32)), -0.4, 0.0), -0.5, 0.5)
    regime_table_keys = jax.random.split(jax.random.fold_in(splits[2], 1), N_TILE * (N_SECT * N_EMU) * (CX * CY) // (CX * CY))
    regime_table_turns = jax.random.permutation(jax.random.fold_in(splits[2], 3), N_TILE * (N_SECT * N_EMU) * (CX * CY) // (CX * CY))
    regime_table = jax.vmap(lambda own, number: assign_block(jax.random.fold_in(splits[2], 2), own, number, CX * CY, REG, 1, CAP, 2))(regime_table_keys, regime_table_turns).reshape((N_TILE, N_SECT * N_EMU, CX * CY, 1))
    emu_lift = noise(splits[3], (REG, CH, VARS), VARS ** -0.5, 2.0, ((0, 4),))
    emu_conv = noise(splits[4], (REG, LAYERS, 3, CH, CH), (3 * CH) ** -0.5, 0.3125, ((0, 4),))
    emu_output = noise(splits[5], (REG, VARS, CH), CH ** -0.5, 0.5, ((0, 4),))
    return {"state": state, "winds": winds, "regime_table": regime_table, "emu_lift": emu_lift, "emu_conv": emu_conv, "emu_output": emu_output}


def upwind_flux(speed, before, center, after, beyond):
    central = 7.0 * (center + after) - (before + beyond)
    damping = (beyond - before) - 3.0 * (after - center)
    return (speed * central + jnp.abs(speed) * damping) / 12.0


def tendency_global(field, winds):
    east = winds[0][None]
    north = winds[1][None]
    flux_x = upwind_flux(east, jnp.roll(field, 1, 2), field, jnp.roll(field, -1, 2), jnp.roll(field, -2, 2))
    flux_y = upwind_flux(north, jnp.roll(field, 1, 3), field, jnp.roll(field, -1, 3), jnp.roll(field, -2, 3))
    return -(flux_x - jnp.roll(flux_x, 1, 2)) - (flux_y - jnp.roll(flux_y, 1, 3))


def advance(field, spatial):
    first = field + spatial(field)
    second = 0.75 * field + 0.25 * (first + spatial(first))
    return field / 3.0 + (2.0 / 3.0) * (second + spatial(second))


def selection(regimes, count_regimes, capacity):
    member = (regimes[None, :] == jnp.arange(count_regimes, dtype=jnp.int32)[:, None]).astype(jnp.int32)
    position = jnp.cumsum(member, axis=1) - 1
    slots = jnp.arange(capacity, dtype=jnp.int32)
    picked = (member[:, None, :] == 1) & (position[:, None, :] == slots[None, :, None])
    return picked.astype(jnp.float32)


def column_network(columns, lift, convs, output_map):
    count_vars = lift.shape[1]
    inputs = columns.reshape(count_vars, -1, columns.shape[1]).astype(jnp.float32)
    levels = inputs.shape[1]
    hidden = jnp.einsum("cv,vls->lcs", lift.astype(jnp.float32), inputs)
    for layer_index in range(convs.shape[0]):
        spacing = 2 ** layer_index
        active = jax.nn.silu(hidden).astype(jnp.bfloat16).astype(jnp.float32)
        padded = jnp.pad(active, ((spacing, spacing), (0, 0), (0, 0)))
        for offset_index in range(3):
            window = padded[offset_index * spacing: offset_index * spacing + levels]
            hidden = hidden + jnp.einsum("oc,lcs->los", convs[layer_index, offset_index].astype(jnp.float32), window)
    rounded = hidden.astype(jnp.bfloat16).astype(jnp.float32)
    result = jnp.einsum("vc,lcs->vls", output_map.astype(jnp.float32), rounded)
    return result.reshape(-1, columns.shape[1]).astype(jnp.bfloat16)


def reference(state, winds, regime_table, emu_lift, emu_conv, emu_output):
    count_vars, levels, total_x, total_y = state.shape
    tiles, blocks_y, cells, unused_dim = regime_table.shape
    width_x = total_x // tiles
    width_y = total_y // blocks_y
    count_regimes = emu_lift.shape[0]
    regimes = regime_table.reshape(tiles * blocks_y, cells)

    def spatial(value):
        return tendency_global(value, winds)

    def per_block(pair):
        block_data, block_regimes = pair
        picked = selection(block_regimes, count_regimes, CAP)
        packed = jnp.einsum("ac,rpc->rap", block_data.astype(jnp.float32), picked).astype(jnp.bfloat16)
        results = jax.vmap(column_network)(packed, emu_lift, emu_conv, emu_output)
        return jnp.einsum("rap,rpc->ac", results.astype(jnp.float32), picked)

    field = state
    for step_index in range(STEPS):
        field = advance(field, spatial)
        grouped = field.reshape(count_vars, levels, tiles, width_x, blocks_y, width_y)
        grouped = grouped.transpose(2, 4, 0, 1, 3, 5).reshape(tiles * blocks_y, count_vars * levels, cells)
        tendency = lax.map(per_block, (grouped.astype(jnp.bfloat16), regimes))
        tendency = tendency.reshape(tiles, blocks_y, count_vars, levels, width_x, width_y)
        tendency = tendency.transpose(2, 3, 0, 4, 1, 5).reshape(state.shape)
        field = field + tendency
    return field
```

```python
import functools

import jax
import jax.numpy as jnp
from jax import lax
from jax.experimental import pallas as pl
from jax.experimental.pallas import tpu as pltpu
from jax.sharding import PartitionSpec as P

MESH = pl.DeviceIdType.MESH
STEPS = 2
SIDE = 16
LANES = 128
VARS = 8
LEVELS = 16
REGIMES = 4
LAYERS = 4
TILE = 32
TILES = 11
SLOTS = TILES * TILE
PAD_SLOTS = 384
X0, Y0 = 6, 8
PAD_X, PAD_Y = 28, 32
DIRECTIONS = ((1, 0), (-1, 0), (0, 1), (0, -1), (1, 1), (1, -1), (-1, 1), (-1, -1))
BF16 = jnp.bfloat16
F32 = jnp.float32


def dot(a, b):
    return jnp.dot(a, b, preferred_element_type=F32)


def dot_nt(a, b):
    return lax.dot_general(a, b, (((1,), (1,)), ((), ())), preferred_element_type=F32)


def iota(shape, dim):
    return lax.broadcasted_iota(jnp.int32, shape, dim)


def field_rows(dx, dy):
    return 96 if dy == 0 else 128 if dx == 0 else 32


def wind_rows(dx, dy):
    return 16 if dx and dy else 32


def sent_box(dx, dy):
    if dx and dy:
        xs = slice(X0 + 12, X0 + 16) if dx > 0 else slice(X0, X0 + 4)
    elif dx:
        xs = slice(X0 + 10, X0 + 16) if dx > 0 else slice(X0, X0 + 6)
    else:
        xs = slice(X0, X0 + SIDE)
    ys = slice(Y0, Y0 + SIDE)
    if dy:
        ys = slice(Y0 + 8, Y0 + 16) if dy > 0 else slice(Y0, Y0 + 8)
    return xs, ys


def landing_box(dx, dy):
    xs, ys = sent_box(dx, dy)
    return (
        slice(xs.start - SIDE * dx, xs.stop - SIDE * dx),
        slice(ys.start - SIDE * dy, ys.stop - SIDE * dy),
    )


def wind_groups(dx, dy):
    ys = sent_box(dx, dy)[1]
    if dx == 0:
        return [(slice(X0 + 4 * g, X0 + 4 * g + 4), ys) for g in range(4)]
    base = X0 + 8 if dx > 0 else X0
    return [(slice(base + 2 * g, base + 2 * g + 2), ys) for g in range(4)]


def local_tendency(src, east, north, flux, xs, ys):
    nx, ny = xs.stop - xs.start, ys.stop - ys.start

    def face_flux(speed, before, center, after, beyond):
        both = 2.0 * (center + after)
        up = jnp.maximum(speed, 0.0)
        down = jnp.minimum(speed, 0.0)
        return up * (both + 3.0 * center - before) + down * (both + 3.0 * after - beyond)

    along_x = src[xs.start - 2 : xs.stop + 2, ys, :]
    flux_x = face_flux(
        east[xs.start - 1 : xs.stop, ys, :],
        along_x[0 : nx + 1],
        along_x[1 : nx + 2],
        along_x[2 : nx + 3],
        along_x[3 : nx + 4],
    )
    total = flux_x[:nx] - flux_x[1:]
    faces = slice(ys.start - 1, ys.stop)
    flux[0:nx, 0 : ny + 1, :] = face_flux(
        north[xs, faces, :],
        src[xs, faces.start - 1 : faces.stop - 1, :],
        src[xs, faces, :],
        src[xs, faces.start + 1 : faces.stop + 1, :],
        src[xs, faces.start + 2 : faces.stop + 2, :],
    )
    return total + (flux[0:nx, 0:ny, :] - flux[0:nx, 1 : ny + 1, :])


def kernel(
    state_ref, wind_ref, regime_ref, small_ref, conv_ref, out_ref,
    field, first, second, east, north, flux,
    send_x, recv_x, send_y, recv_y, send_c, recv_c,
    conv, small, lift_map, out_map, spread, pick, unpick, ordered, answers,
    halo_send, halo_recv, weight_send, weight_recv, small_send, small_recv, own_sem,
):
    count_tile, count_sect, count_emu = (lax.axis_size(n) for n in ("tile", "sect", "emu"))
    tile, sect, emu = (lax.axis_index(n) for n in ("tile", "sect", "emu"))
    along_y = sect * count_emu + emu
    total_y = count_sect * count_emu

    def neighbour(dx, dy):
        y = lax.rem(along_y + (dy + total_y), total_y)
        return (lax.rem(tile + (dx + count_tile), count_tile), y // count_emu, lax.rem(y, count_emu))

    half = count_tile // 2
    far_tile = lax.rem(tile + half, count_tile)
    core, chip = lax.rem(sect, 2), sect // 2
    partners = (
        (tile, chip * 2 + (1 - core), emu),
        (tile, (1 - chip) * 2 + core, emu),
        (far_tile, (1 - chip) * 2 + (1 - core), emu),
    )
    neighbours = [neighbour(dx, dy) for dx, dy in DIRECTIONS]

    barrier = pltpu.get_barrier_semaphore()
    for device in (*neighbours, *partners):
        pl.semaphore_signal(barrier, inc=1, device_id=device, device_id_type=MESH)

    own_copies = [
        pltpu.make_async_copy(conv_ref, conv.at[sect], own_sem.at[0]),
        pltpu.make_async_copy(small_ref, small.at[sect], own_sem.at[1]),
    ]
    for copy in own_copies:
        copy.start()

    row, column = iota((LANES, 8 * LANES), 0), iota((LANES, 8 * LANES), 1)
    group, part = column // (2 * LANES), (column // LANES) % 2
    chosen = (row // LEVELS == part * 4 + group) & (row % LEVELS == column % LEVELS)
    spread[...] = jnp.where(chosen, 1.0, 0.0).astype(BF16)
    wide = dot(wind_ref[...], spread[...])
    for g in range(4):
        at = (slice(X0 + 4 * g, X0 + 4 * g + 4), slice(Y0, Y0 + SIDE), slice(None))
        east[at] = wide[:, 256 * g : 256 * g + 128].reshape(4, SIDE, LANES)
        north[at] = wide[:, 256 * g + 128 : 256 * g + 256].reshape(4, SIDE, LANES)
    field[X0 : X0 + SIDE, Y0 : Y0 + SIDE, :] = state_ref[...].reshape(SIDE, SIDE, LANES)

    def buffers(step, k):
        dx, dy = DIRECTIONS[k]
        if dy == 0:
            return send_x.at[step, k], recv_x.at[step, k]
        if dx == 0:
            return send_y.at[step, k - 2], recv_y.at[step, k - 2]
        return send_c.at[step, k - 4], recv_c.at[step, k - 4]

    def halo_copy(step, k):
        sent, received = buffers(step, k)
        rows = field_rows(*DIRECTIONS[k]) + (wind_rows(*DIRECTIONS[k]) if step == 0 else 0)
        return pltpu.make_async_remote_copy(
            src_ref=sent.at[0:rows],
            dst_ref=received.at[0:rows],
            send_sem=halo_send.at[step, k],
            recv_sem=halo_recv.at[step, k],
            device_id=neighbours[k],
            device_id_type=MESH,
        )

    def pack(step):
        for k, (dx, dy) in enumerate(DIRECTIONS):
            sent, _ = buffers(step, k)
            xs, ys = sent_box(dx, dy)
            rows = field_rows(dx, dy)
            sent[0:rows, :] = field[xs, ys, :].reshape(rows, LANES).astype(BF16)
            if step == 0:
                more = wind_rows(dx, dy)
                quarter = iota((more, LANES), 1) // LEVELS
                packed = jnp.zeros((more, LANES), F32)
                for c, winds in enumerate((east, north)):
                    for g, (gx, gy) in enumerate(wind_groups(dx, dy)):
                        if dx and dy and g // 2 != (1 if dx > 0 else 0):
                            continue
                        piece = winds[gx, gy, :].reshape(more, LANES)
                        packed = jnp.where(quarter == c * 4 + g, piece, packed)
                sent[rows : rows + more, :] = packed.astype(BF16)

    def unpack(step):
        for k, (dx, dy) in enumerate(DIRECTIONS):
            _, received = buffers(step, k)
            xs, ys = landing_box(dx, dy)
            rows = field_rows(dx, dy)
            nx, ny = xs.stop - xs.start, ys.stop - ys.start
            field[xs, ys, :] = received[0:rows, :].astype(F32).reshape(nx, ny, LANES)
            if step == 0:
                more = wind_rows(dx, dy)
                wide = dot(received[rows : rows + more, :], spread[...])
                for g, (gx, gy) in enumerate(wind_groups(dx, dy)):
                    if dx and dy and g // 2 != (1 if dx > 0 else 0):
                        continue
                    x_from, x_to = gx.start - SIDE * dx, gx.stop - SIDE * dx
                    if x_from < 0 or x_to > PAD_X:
                        continue
                    at = (slice(x_from, x_to), ys, slice(None))
                    shape = (x_to - x_from, ny, LANES)
                    east[at] = wide[:, 256 * g : 256 * g + 128].reshape(shape)
                    north[at] = wide[:, 256 * g + 128 : 256 * g + 256].reshape(shape)

    pack(0)
    pl.semaphore_wait(barrier, len(neighbours) + len(partners))
    halo = [halo_copy(0, k) for k in range(8)]
    for copy in halo:
        copy.start()

    def weight_copies(j):
        copies = [
            pltpu.make_async_remote_copy(
                src_ref=small_ref,
                dst_ref=small.at[sect],
                send_sem=small_send.at[j],
                recv_sem=small_recv.at[j],
                device_id=partners[j],
                device_id_type=MESH,
            )
        ]
        for layer in range(LAYERS):
            part = pl.ds(3 * layer, 3)
            copies.append(
                pltpu.make_async_remote_copy(
                    src_ref=conv_ref.at[part],
                    dst_ref=conv.at[sect, part],
                    send_sem=weight_send.at[j, layer],
                    recv_sem=weight_recv.at[j, layer],
                    device_id=partners[j],
                    device_id_type=MESH,
                )
            )
        return copies

    weights = [weight_copies(j) for j in range(3)]
    for i in range(LAYERS + 1):
        for j in range(3):
            weights[j][i].start()

    regimes = regime_ref[...]
    member = jnp.where(regimes == iota((256, LANES), 1), 1.0, 0.0)
    earlier = jnp.where(iota((256, 256), 1) < iota((256, 256), 0), 1.0, 0.0).astype(BF16)
    place = member * dot(earlier, member.astype(BF16))
    counts = jnp.sum(member, axis=0, keepdims=True)
    tiles = jnp.floor((counts + (TILE - 1)) * (1.0 / TILE))
    before = jnp.where(iota((LANES, LANES), 0) < iota((LANES, LANES), 1), 1.0, 0.0).astype(BF16)
    starts = dot(jnp.broadcast_to(tiles, (8, LANES)).astype(BF16), before)[0:1, :]
    start = member * starts
    slot_column = jnp.sum(place + TILE * start, axis=1, keepdims=True)
    ones = jnp.ones((8, LANES), BF16)
    slot_row = (dot_nt(ones, place.astype(BF16)) + TILE * dot_nt(ones, start.astype(BF16)))[0:1, :]
    unpick[...] = jnp.where(
        slot_column == iota((256, PAD_SLOTS), 1).astype(F32), 1.0, 0.0
    ).astype(BF16)
    pick[...] = jnp.where(
        slot_row == iota((PAD_SLOTS, 256), 0).astype(F32), 1.0, 0.0
    ).astype(BF16)
    answers[SLOTS:, :] = jnp.zeros((PAD_SLOTS - SLOTS, LANES), BF16)
    ends = []
    used = 0
    for r in range(REGIMES - 1):
        named = jnp.sum(jnp.where(regimes == r, 1, 0))
        used = used + (named + (TILE - 1)) // TILE
        ends.append(used)

    def network(tile_index, carry):
        regime = sum(jnp.where(tile_index >= end, 1, 0) for end in ends)
        at = pl.ds(pl.multiple_of(tile_index * TILE, TILE), TILE)
        columns = ordered[at, :]
        level_of = iota((TILE, LANES), 1) % LEVELS
        zero = jnp.zeros((TILE, LANES), BF16)
        masked = [jnp.where(level_of == m, columns, zero) for m in range(LEVELS)]
        lift = lift_map[regime]
        square = jnp.zeros((LANES, LANES), BF16)

        def beside(a, b):
            return jnp.concatenate([a, b], axis=1)

        def over(a, b):
            return jnp.concatenate([a, b], axis=0)

        rows = jnp.concatenate([beside(masked[m], masked[m + 1]) for m in range(0, LEVELS, 2)], axis=0)
        lifted = dot(rows, over(beside(lift, square), beside(square, lift)))
        hidden = [
            lifted[(m // 2) * TILE : (m // 2 + 1) * TILE, (m % 2) * LANES : (m % 2 + 1) * LANES]
            for m in range(LEVELS)
        ]
        for layer in range(LAYERS):
            spacing = 2**layer
            below, centre, above = (conv[regime, 3 * layer + t] for t in range(3))
            active = []
            for m in range(LEVELS):
                u = 0.5 * hidden[m]
                active.append((u + u * jnp.tanh(u)).astype(BF16))
            low = [m for m in range(LEVELS) if (m // spacing) % 2 == 0]
            inner = jnp.concatenate([beside(active[m], active[m + spacing]) for m in low], axis=0)
            result = dot_nt(inner, over(beside(centre, above), beside(below, centre)))
            if 2 * spacing < LEVELS:
                outer = jnp.concatenate(
                    [
                        beside(
                            active[m - spacing] if m >= spacing else zero,
                            active[m + 2 * spacing] if m + 2 * spacing < LEVELS else zero,
                        )
                        for m in low
                    ],
                    axis=0,
                )
                result = result + dot_nt(outer, over(beside(below, square), beside(square, above)))
            for p, m in enumerate(low):
                rows_of = slice(p * TILE, (p + 1) * TILE)
                hidden[m] = hidden[m] + result[rows_of, :LANES]
                hidden[m + spacing] = hidden[m + spacing] + result[rows_of, LANES:]
        rounded = [h.astype(BF16) for h in hidden]
        rows = jnp.concatenate([beside(rounded[m], rounded[m + 1]) for m in range(0, LEVELS, 2)], axis=0)
        mapped = out_map[regime]
        result = dot_nt(rows, over(beside(mapped, square), beside(square, mapped)))
        answer = jnp.zeros((TILE, LANES), F32)
        for m in range(LEVELS):
            piece = result[(m // 2) * TILE : (m // 2 + 1) * TILE, (m % 2) * LANES : (m % 2 + 1) * LANES]
            answer = jnp.where(level_of == m, piece, answer)
        answers[at, :] = answer.astype(BF16)
        return carry

    own = (slice(X0, X0 + SIDE), slice(Y0, Y0 + SIDE), slice(None))
    for step in range(STEPS):
        if step:
            pack(step)
            halo = [halo_copy(step, k) for k in range(8)]
            for copy in halo:
                copy.start()
        for copy in halo:
            copy.wait_recv()
        unpack(step)
        xs, ys = slice(X0 - 4, X0 + SIDE + 4), slice(Y0 - 4, Y0 + SIDE + 4)
        first[xs, ys, :] = field[xs, ys, :] + (1.0 / 6.0) * local_tendency(
            field, east, north, flux, xs, ys
        )
        xs, ys = slice(X0 - 2, X0 + SIDE + 2), slice(Y0 - 2, Y0 + SIDE + 2)
        second[xs, ys, :] = (
            0.75 * field[xs, ys, :]
            + 0.25 * first[xs, ys, :]
            + (0.25 / 6.0) * local_tendency(first, east, north, flux, xs, ys)
        )
        xs, ys = own[0], own[1]
        dyn = (
            (1.0 / 3.0) * field[own]
            + (2.0 / 3.0) * second[own]
            + (1.0 / 9.0) * local_tendency(second, east, north, flux, xs, ys)
        ).reshape(SIDE * SIDE, LANES)
        ordered[...] = dot(pick[0:SLOTS, :], dyn.astype(BF16)).astype(BF16)
        if step == 0:
            for copy in own_copies:
                copy.wait()
            for j in range(3):
                for copy in weights[j]:
                    copy.wait_recv()
            row, column = iota((LANES, 16), 0), iota((LANES, 16), 1)
            to_lift = jnp.where(row // LEVELS == column, 1.0, 0.0).astype(BF16)
            to_out = jnp.where(row // LEVELS + VARS == column, 1.0, 0.0).astype(BF16)
            for r in range(REGIMES):
                lift_map[r] = dot(to_lift, small[r]).astype(BF16)
                out_map[r] = dot(to_out, small[r]).astype(BF16)
        lax.fori_loop(0, TILES, network, 0)
        final = dyn + dot(unpick[...], answers[...])
        if step == STEPS - 1:
            out_ref[...] = final
        else:
            field[own] = final.reshape(SIDE, SIDE, LANES)
        for copy in halo:
            copy.wait_send()
    for j in range(3):
        for copy in weights[j]:
            copy.wait_send()


def per_device(state, winds, regime_table, emu_lift, emu_conv, emu_output):
    cells = SIDE * SIDE
    columns = state.transpose(2, 3, 0, 1).reshape(cells, LANES)
    packed = (
        winds.astype(BF16)
        .reshape(2, LEVELS, 4, 4, SIDE)
        .transpose(3, 4, 0, 2, 1)
        .reshape(4 * SIDE, LANES)
    )
    regimes = regime_table.reshape(cells, 1)
    small = jnp.concatenate([emu_lift[0].T, emu_output[0]], axis=0)
    taps = emu_conv.reshape(3 * LAYERS, LANES, LANES)
    padded = pltpu.VMEM((PAD_X, PAD_Y, LANES), F32)
    dma = pltpu.SemaphoreType.DMA
    result = pl.pallas_call(
        kernel,
        out_shape=jax.ShapeDtypeStruct((cells, LANES), F32),
        in_specs=[pl.BlockSpec(memory_space=pltpu.VMEM)] * 3
        + [pl.BlockSpec(memory_space=pltpu.VMEM), pl.BlockSpec(memory_space=pl.ANY)],
        out_specs=pl.BlockSpec(memory_space=pltpu.VMEM),
        scratch_shapes=[
            padded, padded, padded, padded, padded,
            pltpu.VMEM((24, PAD_Y, LANES), F32),
            pltpu.VMEM((STEPS, 2, 128, LANES), BF16),
            pltpu.VMEM((STEPS, 2, 128, LANES), BF16),
            pltpu.VMEM((STEPS, 2, 160, LANES), BF16),
            pltpu.VMEM((STEPS, 2, 160, LANES), BF16),
            pltpu.VMEM((STEPS, 4, 48, LANES), BF16),
            pltpu.VMEM((STEPS, 4, 48, LANES), BF16),
            pltpu.VMEM((REGIMES, 3 * LAYERS, LANES, LANES), BF16),
            pltpu.VMEM((REGIMES, 16, LANES), BF16),
            pltpu.VMEM((REGIMES, LANES, LANES), BF16),
            pltpu.VMEM((REGIMES, LANES, LANES), BF16),
            pltpu.VMEM((LANES, 8 * LANES), BF16),
            pltpu.VMEM((PAD_SLOTS, cells), BF16),
            pltpu.VMEM((cells, PAD_SLOTS), BF16),
            pltpu.VMEM((SLOTS, LANES), BF16),
            pltpu.VMEM((PAD_SLOTS, LANES), BF16),
            dma((STEPS, 8)), dma((STEPS, 8)),
            dma((3, LAYERS)), dma((3, LAYERS)),
            dma((3,)), dma((3,)),
            dma((2,)),
        ],
        compiler_params=pltpu.CompilerParams(
            collective_id=0, has_side_effects=True, vmem_limit_bytes=32 * 2**20
        ),
    )(columns, packed, regimes, small, taps)
    return result.reshape(SIDE, SIDE, VARS, LEVELS).transpose(2, 3, 0, 1)


def solution(mesh):
    in_specs = (
        P(None, None, "tile", ("sect", "emu")),
        P(None, None, "tile", ("sect", "emu")),
        P("tile", ("sect", "emu"), None, None),
        P("sect", None, None),
        P("sect", None, None, None, None),
        P("sect", None, None),
    )
    out_specs = P(None, None, "tile", ("sect", "emu"))
    return jax.shard_map(
        per_device, mesh=mesh, in_specs=in_specs, out_specs=out_specs, check_vma=False
    )
```

```python
import functools

import jax
import jax.numpy as jnp
from jax import lax
from jax.experimental import pallas as pl
from jax.experimental.pallas import tpu as pltpu
from jax.sharding import PartitionSpec as P

MESH = pl.DeviceIdType.MESH
STEPS = 2
SIDE = 16
LANES = 128
VARS = 8
LEVELS = 16
REGIMES = 4
LAYERS = 4
TILE = 32
TILES = 12
GROUP = 4
SLOTS = TILES * TILE
X0, Y0 = 6, 8
PAD_X, PAD_Y = 28, 32
DIRECTIONS = ((1, 0), (-1, 0), (0, 1), (0, -1), (1, 1), (1, -1), (-1, 1), (-1, -1))
BF16 = jnp.bfloat16
F32 = jnp.float32


def dot(a, b):
    return jnp.dot(a, b, preferred_element_type=F32)


def dot_nt(a, b):
    return lax.dot_general(a, b, (((1,), (1,)), ((), ())), preferred_element_type=F32)


def iota(shape, dim):
    return lax.broadcasted_iota(jnp.int32, shape, dim)


def field_rows(dx, dy):
    return 96 if dy == 0 else 128 if dx == 0 else 32


def wind_rows(dx, dy):
    return 16 if dx and dy else 32


def sent_box(dx, dy):
    if dx and dy:
        xs = slice(X0 + 12, X0 + 16) if dx > 0 else slice(X0, X0 + 4)
    elif dx:
        xs = slice(X0 + 10, X0 + 16) if dx > 0 else slice(X0, X0 + 6)
    else:
        xs = slice(X0, X0 + SIDE)
    ys = slice(Y0, Y0 + SIDE)
    if dy:
        ys = slice(Y0 + 8, Y0 + 16) if dy > 0 else slice(Y0, Y0 + 8)
    return xs, ys


def landing_box(dx, dy):
    xs, ys = sent_box(dx, dy)
    return (
        slice(xs.start - SIDE * dx, xs.stop - SIDE * dx),
        slice(ys.start - SIDE * dy, ys.stop - SIDE * dy),
    )


def wind_groups(dx, dy):
    ys = sent_box(dx, dy)[1]
    if dx == 0:
        return [(slice(X0 + 4 * g, X0 + 4 * g + 4), ys) for g in range(4)]
    base = X0 + 8 if dx > 0 else X0
    return [(slice(base + 2 * g, base + 2 * g + 2), ys) for g in range(4)]


def local_tendency(src, east, north, flux, xs, ys):
    nx, ny = xs.stop - xs.start, ys.stop - ys.start

    def face_flux(speed, before, center, after, beyond):
        both = 2.0 * (center + after)
        up = jnp.maximum(speed, 0.0)
        down = jnp.minimum(speed, 0.0)
        return up * (both + 3.0 * center - before) + down * (both + 3.0 * after - beyond)

    along_x = src[xs.start - 2 : xs.stop + 2, ys, :]
    flux_x = face_flux(
        east[xs.start - 1 : xs.stop, ys, :],
        along_x[0 : nx + 1],
        along_x[1 : nx + 2],
        along_x[2 : nx + 3],
        along_x[3 : nx + 4],
    )
    total = flux_x[:nx] - flux_x[1:]
    faces = slice(ys.start - 1, ys.stop)
    flux[0:nx, 0 : ny + 1, :] = face_flux(
        north[xs, faces, :],
        src[xs, faces.start - 1 : faces.stop - 1, :],
        src[xs, faces, :],
        src[xs, faces.start + 1 : faces.stop + 1, :],
        src[xs, faces.start + 2 : faces.stop + 2, :],
    )
    return total + (flux[0:nx, 0:ny, :] - flux[0:nx, 1 : ny + 1, :])


def kernel(
    state_ref, wind_ref, regime_ref, small_ref, conv_ref, out_ref,
    field, first, second, east, north, flux,
    send_x, recv_x, send_y, recv_y, send_c, recv_c,
    conv, small, lift_map, out_map, spread, pick, unpick, ordered, answers,
    halo_send, halo_recv, weight_send, weight_recv, small_send, small_recv,
):
    count_tile, count_sect, count_emu = (lax.axis_size(n) for n in ("tile", "sect", "emu"))
    tile, sect, emu = (lax.axis_index(n) for n in ("tile", "sect", "emu"))
    along_y = sect * count_emu + emu
    total_y = count_sect * count_emu

    def neighbour(dx, dy):
        y = lax.rem(along_y + (dy + total_y), total_y)
        return (lax.rem(tile + (dx + count_tile), count_tile), y // count_emu, lax.rem(y, count_emu))

    half = count_tile // 2
    far_tile = lax.rem(tile + half, count_tile)
    core, chip = lax.rem(sect, 2), sect // 2
    partners = (
        (tile, chip * 2 + (1 - core), emu),
        (tile, (1 - chip) * 2 + core, emu),
        (far_tile, (1 - chip) * 2 + (1 - core), emu),
    )
    neighbours = [neighbour(dx, dy) for dx, dy in DIRECTIONS]

    barrier = pltpu.get_barrier_semaphore()
    for device in (*neighbours, *partners):
        pl.semaphore_signal(barrier, inc=1, device_id=device, device_id_type=MESH)

    conv[sect] = 0.5 * conv_ref[...]
    small[sect] = small_ref[...]

    row, column = iota((LANES, 8 * LANES), 0), iota((LANES, 8 * LANES), 1)
    group, part = column // (2 * LANES), (column // LANES) % 2
    chosen = (row // LEVELS == part * 4 + group) & (row % LEVELS == column % LEVELS)
    spread[...] = jnp.where(chosen, 1.0, 0.0).astype(BF16)
    wide = dot(wind_ref[...], spread[...])
    for g in range(4):
        at = (slice(X0 + 4 * g, X0 + 4 * g + 4), slice(Y0, Y0 + SIDE), slice(None))
        east[at] = wide[:, 256 * g : 256 * g + 128].reshape(4, SIDE, LANES)
        north[at] = wide[:, 256 * g + 128 : 256 * g + 256].reshape(4, SIDE, LANES)
    field[X0 : X0 + SIDE, Y0 : Y0 + SIDE, :] = state_ref[...].reshape(SIDE, SIDE, LANES)

    def buffers(step, k):
        dx, dy = DIRECTIONS[k]
        if dy == 0:
            return send_x.at[step, k], recv_x.at[step, k]
        if dx == 0:
            return send_y.at[step, k - 2], recv_y.at[step, k - 2]
        return send_c.at[step, k - 4], recv_c.at[step, k - 4]

    def halo_copy(step, k):
        sent, received = buffers(step, k)
        rows = field_rows(*DIRECTIONS[k]) + (wind_rows(*DIRECTIONS[k]) if step == 0 else 0)
        return pltpu.make_async_remote_copy(
            src_ref=sent.at[0:rows],
            dst_ref=received.at[0:rows],
            send_sem=halo_send.at[step, k],
            recv_sem=halo_recv.at[step, k],
            device_id=neighbours[k],
            device_id_type=MESH,
        )

    def pack(step):
        for k, (dx, dy) in enumerate(DIRECTIONS):
            sent, _ = buffers(step, k)
            xs, ys = sent_box(dx, dy)
            rows = field_rows(dx, dy)
            sent[0:rows, :] = field[xs, ys, :].reshape(rows, LANES).astype(BF16)
            if step == 0:
                more = wind_rows(dx, dy)
                quarter = iota((more, LANES), 1) // LEVELS
                packed = jnp.zeros((more, LANES), F32)
                for c, winds in enumerate((east, north)):
                    for g, (gx, gy) in enumerate(wind_groups(dx, dy)):
                        if dx and dy and g // 2 != (1 if dx > 0 else 0):
                            continue
                        piece = winds[gx, gy, :].reshape(more, LANES)
                        packed = jnp.where(quarter == c * 4 + g, piece, packed)
                sent[rows : rows + more, :] = packed.astype(BF16)

    def unpack(step):
        for k, (dx, dy) in enumerate(DIRECTIONS):
            _, received = buffers(step, k)
            xs, ys = landing_box(dx, dy)
            rows = field_rows(dx, dy)
            nx, ny = xs.stop - xs.start, ys.stop - ys.start
            field[xs, ys, :] = received[0:rows, :].astype(F32).reshape(nx, ny, LANES)
            if step == 0:
                more = wind_rows(dx, dy)
                wide = dot(received[rows : rows + more, :], spread[...])
                for g, (gx, gy) in enumerate(wind_groups(dx, dy)):
                    if dx and dy and g // 2 != (1 if dx > 0 else 0):
                        continue
                    x_from, x_to = gx.start - SIDE * dx, gx.stop - SIDE * dx
                    if x_from < 0 or x_to > PAD_X:
                        continue
                    at = (slice(x_from, x_to), ys, slice(None))
                    shape = (x_to - x_from, ny, LANES)
                    east[at] = wide[:, 256 * g : 256 * g + 128].reshape(shape)
                    north[at] = wide[:, 256 * g + 128 : 256 * g + 256].reshape(shape)

    pack(0)
    pl.semaphore_wait(barrier, len(neighbours) + len(partners))
    halo = [halo_copy(0, k) for k in range(8)]
    for copy in halo:
        copy.start()

    def weight_copies(j):
        copies = [
            pltpu.make_async_remote_copy(
                src_ref=small.at[sect],
                dst_ref=small.at[sect],
                send_sem=small_send.at[j],
                recv_sem=small_recv.at[j],
                device_id=partners[j],
                device_id_type=MESH,
            )
        ]
        for layer in range(LAYERS):
            part = pl.ds(3 * layer, 3)
            copies.append(
                pltpu.make_async_remote_copy(
                    src_ref=conv.at[sect, part],
                    dst_ref=conv.at[sect, part],
                    send_sem=weight_send.at[j, layer],
                    recv_sem=weight_recv.at[j, layer],
                    device_id=partners[j],
                    device_id_type=MESH,
                )
            )
        return copies

    weights = [weight_copies(j) for j in range(3)]
    for i in range(LAYERS + 1):
        for j in range(3):
            weights[j][i].start()

    regimes = regime_ref[...]
    member = jnp.where(regimes == iota((256, LANES), 1), 1.0, 0.0)
    earlier = jnp.where(iota((256, 256), 1) < iota((256, 256), 0), 1.0, 0.0).astype(BF16)
    place = member * dot(earlier, member.astype(BF16))
    counts = jnp.sum(member, axis=0, keepdims=True)
    tiles = jnp.floor((counts + (TILE - 1)) * (1.0 / TILE))
    before = jnp.where(iota((LANES, LANES), 0) < iota((LANES, LANES), 1), 1.0, 0.0).astype(BF16)
    starts = dot(jnp.broadcast_to(tiles, (8, LANES)).astype(BF16), before)[0:1, :]
    start = member * starts
    slot_column = jnp.sum(place + TILE * start, axis=1, keepdims=True)
    ones = jnp.ones((8, LANES), BF16)
    slot_row = (dot_nt(ones, place.astype(BF16)) + TILE * dot_nt(ones, start.astype(BF16)))[0:1, :]
    unpick[...] = jnp.where(
        slot_column == iota((256, SLOTS), 1).astype(F32), 1.0, 0.0
    ).astype(BF16)
    pick[...] = jnp.where(
        slot_row == iota((SLOTS, 256), 0).astype(F32), 1.0, 0.0
    ).astype(BF16)
    ends = []
    used = 0
    for r in range(REGIMES - 1):
        named = jnp.sum(jnp.where(regimes == r, 1, 0))
        used = used + (named + (TILE - 1)) // TILE
        ends.append(used)

    level_of = iota((TILE, LANES), 1) % LEVELS
    zero = jnp.zeros((TILE, LANES), BF16)
    square = jnp.zeros((LANES, LANES), BF16)

    def beside(a, b):
        return jnp.concatenate([a, b], axis=1)

    def over(a, b):
        return jnp.concatenate([a, b], axis=0)

    def in_pairs(levels):
        return jnp.concatenate([beside(levels[m], levels[m + 1]) for m in range(0, LEVELS, 2)], axis=0)

    def out_of_pairs(rows):
        return [
            rows[(m // 2) * TILE : (m // 2 + 1) * TILE, (m % 2) * LANES : (m % 2 + 1) * LANES]
            for m in range(LEVELS)
        ]

    def lifted(regime, at):
        columns = ordered[at, :]
        masked = [jnp.where(level_of == m, columns, zero) for m in range(LEVELS)]
        lift = lift_map[regime]
        return out_of_pairs(dot(in_pairs(masked), over(beside(lift, square), beside(square, lift))))

    def convolved(regime, layer, active):
        spacing = 2**layer
        below, centre, above = (conv[regime, 3 * layer + t] for t in range(3))
        low = [m for m in range(LEVELS) if (m // spacing) % 2 == 0]
        pieces = [jnp.concatenate([active[m] for m in low], axis=0)]
        pieces.append(jnp.concatenate([active[m + spacing] for m in low], axis=0))
        taps = over(beside(centre, above), beside(below, centre))
        if 2 * spacing < LEVELS:
            pieces.append(
                jnp.concatenate([active[m - spacing] if m >= spacing else zero for m in low], axis=0)
            )
            pieces.append(
                jnp.concatenate(
                    [active[m + 2 * spacing] if m + 2 * spacing < LEVELS else zero for m in low],
                    axis=0,
                )
            )
            taps = beside(taps, over(beside(below, square), beside(square, above)))
        result = dot_nt(jnp.concatenate(pieces, axis=1), taps)
        added = [None] * LEVELS
        for p, m in enumerate(low):
            rows = slice(p * TILE, (p + 1) * TILE)
            added[m] = result[rows, :LANES]
            added[m + spacing] = result[rows, LANES:]
        return added

    def network(group_index, carry):
        places, states = [], []
        for j in range(GROUP):
            tile_index = group_index * GROUP + j
            regime = sum(jnp.where(tile_index >= end, 1, 0) for end in ends)
            at = pl.ds(pl.multiple_of(tile_index * TILE, TILE), TILE)
            places.append((regime, at))
            states.append(lifted(regime, at))
        for layer in range(LAYERS):
            for j in range(GROUP):
                active = []
                for half in states[j]:
                    u = half.astype(BF16)
                    active.append(u + u * jnp.tanh(u))
                added = convolved(places[j][0], layer, active)
                states[j] = [h + a for h, a in zip(states[j], added)]
        for j in range(GROUP):
            regime, at = places[j]
            mapped = out_map[regime]
            rows = in_pairs([h.astype(BF16) for h in states[j]])
            pieces = out_of_pairs(dot_nt(rows, over(beside(mapped, square), beside(square, mapped))))
            answer = jnp.zeros((TILE, LANES), F32)
            for m in range(LEVELS):
                answer = jnp.where(level_of == m, pieces[m], answer)
            answers[at, :] = answer.astype(BF16)
        return carry

    own = (slice(X0, X0 + SIDE), slice(Y0, Y0 + SIDE), slice(None))
    for step in range(STEPS):
        if step:
            pack(step)
            halo = [halo_copy(step, k) for k in range(8)]
            for copy in halo:
                copy.start()
        for copy in halo:
            copy.wait_recv()
        unpack(step)
        xs, ys = slice(X0 - 4, X0 + SIDE + 4), slice(Y0 - 4, Y0 + SIDE + 4)
        first[xs, ys, :] = field[xs, ys, :] + (1.0 / 6.0) * local_tendency(
            field, east, north, flux, xs, ys
        )
        xs, ys = slice(X0 - 2, X0 + SIDE + 2), slice(Y0 - 2, Y0 + SIDE + 2)
        second[xs, ys, :] = (
            0.75 * field[xs, ys, :]
            + 0.25 * first[xs, ys, :]
            + (0.25 / 6.0) * local_tendency(first, east, north, flux, xs, ys)
        )
        xs, ys = own[0], own[1]
        dyn = (
            (1.0 / 3.0) * field[own]
            + (2.0 / 3.0) * second[own]
            + (1.0 / 9.0) * local_tendency(second, east, north, flux, xs, ys)
        ).reshape(SIDE * SIDE, LANES)
        ordered[...] = dot(pick[...], dyn.astype(BF16)).astype(BF16)
        if step == 0:
            for j in range(3):
                for copy in weights[j]:
                    copy.wait_recv()
            row, column = iota((LANES, 16), 0), iota((LANES, 16), 1)
            to_lift = jnp.where(row // LEVELS == column, 0.5, 0.0).astype(BF16)
            to_out = jnp.where(row // LEVELS + VARS == column, 2.0, 0.0).astype(BF16)
            for r in range(REGIMES):
                lift_map[r] = dot(to_lift, small[r]).astype(BF16)
                out_map[r] = dot(to_out, small[r]).astype(BF16)
        lax.fori_loop(0, TILES // GROUP, network, 0)
        final = dyn + dot(unpick[...], answers[...])
        if step == STEPS - 1:
            out_ref[...] = final
        else:
            field[own] = final.reshape(SIDE, SIDE, LANES)
        for copy in halo:
            copy.wait_send()
    for j in range(3):
        for copy in weights[j]:
            copy.wait_send()


def per_device(state, winds, regime_table, emu_lift, emu_conv, emu_output):
    cells = SIDE * SIDE
    columns = state.transpose(2, 3, 0, 1).reshape(cells, LANES)
    packed = (
        winds.astype(BF16)
        .reshape(2, LEVELS, 4, 4, SIDE)
        .transpose(3, 4, 0, 2, 1)
        .reshape(4 * SIDE, LANES)
    )
    regimes = regime_table.reshape(cells, 1)
    small = jnp.concatenate([emu_lift[0].T, emu_output[0]], axis=0)
    taps = emu_conv.reshape(3 * LAYERS, LANES, LANES)
    padded = pltpu.VMEM((PAD_X, PAD_Y, LANES), F32)
    dma = pltpu.SemaphoreType.DMA
    result = pl.pallas_call(
        kernel,
        out_shape=jax.ShapeDtypeStruct((cells, LANES), F32),
        in_specs=[pl.BlockSpec(memory_space=pltpu.VMEM)] * 5,
        out_specs=pl.BlockSpec(memory_space=pltpu.VMEM),
        scratch_shapes=[
            padded, padded, padded, padded, padded,
            pltpu.VMEM((24, PAD_Y, LANES), F32),
            pltpu.VMEM((STEPS, 2, 128, LANES), BF16),
            pltpu.VMEM((STEPS, 2, 128, LANES), BF16),
            pltpu.VMEM((STEPS, 2, 160, LANES), BF16),
            pltpu.VMEM((STEPS, 2, 160, LANES), BF16),
            pltpu.VMEM((STEPS, 4, 48, LANES), BF16),
            pltpu.VMEM((STEPS, 4, 48, LANES), BF16),
            pltpu.VMEM((REGIMES, 3 * LAYERS, LANES, LANES), BF16),
            pltpu.VMEM((REGIMES, 16, LANES), BF16),
            pltpu.VMEM((REGIMES, LANES, LANES), BF16),
            pltpu.VMEM((REGIMES, LANES, LANES), BF16),
            pltpu.VMEM((LANES, 8 * LANES), BF16),
            pltpu.VMEM((SLOTS, cells), BF16),
            pltpu.VMEM((cells, SLOTS), BF16),
            pltpu.VMEM((SLOTS, LANES), BF16),
            pltpu.VMEM((SLOTS, LANES), BF16),
            dma((STEPS, 8)), dma((STEPS, 8)),
            dma((3, LAYERS)), dma((3, LAYERS)),
            dma((3,)), dma((3,)),
        ],
        compiler_params=pltpu.CompilerParams(
            collective_id=0, has_side_effects=True, vmem_limit_bytes=32 * 2**20
        ),
    )(columns, packed, regimes, small, taps)
    return result.reshape(SIDE, SIDE, VARS, LEVELS).transpose(2, 3, 0, 1)


def solution(mesh):
    in_specs = (
        P(None, None, "tile", ("sect", "emu")),
        P(None, None, "tile", ("sect", "emu")),
        P("tile", ("sect", "emu"), None, None),
        P("sect", None, None),
        P("sect", None, None, None, None),
        P("sect", None, None),
    )
    out_specs = P(None, None, "tile", ("sect", "emu"))
    return jax.shard_map(
        per_device, mesh=mesh, in_specs=in_specs, out_specs=out_specs, check_vma=False
    )
```

```python
import functools

import jax
import jax.numpy as jnp
from jax import lax
from jax.experimental import pallas as pl
from jax.experimental.pallas import tpu as pltpu
from jax.sharding import PartitionSpec as P

MESH = pl.DeviceIdType.MESH
STEPS = 2
SIDE = 16
LANES = 128
VARS = 8
LEVELS = 16
REGIMES = 4
LAYERS = 4
TILE = 32
TILES = 11
SLOTS = TILES * TILE
PAD_SLOTS = 384
CORNER = 4
X0, Y0 = 6, 8
PAD_X, PAD_Y = 28, 32
DIRECTIONS = ((1, 1), (1, -1), (-1, 1), (-1, -1), (1, 0), (-1, 0), (0, 1), (0, -1))
BF16 = jnp.bfloat16
F32 = jnp.float32


def dot(a, b):
    return jnp.dot(a, b, preferred_element_type=F32)


def dot_nt(a, b):
    return lax.dot_general(a, b, (((1,), (1,)), ((), ())), preferred_element_type=F32)


def iota(shape, dim):
    return lax.broadcasted_iota(jnp.int32, shape, dim)


def field_rows(dx, dy):
    return 96 if dy == 0 else 128 if dx == 0 else CORNER * CORNER


def wind_rows(dx, dy):
    return 16 if dx and dy else 32


def sent_box(dx, dy):
    deep_x, deep_y = (CORNER, CORNER) if dx and dy else (6, 8)
    xs = slice(X0, X0 + deep_x) if dx < 0 else slice(X0 + SIDE - deep_x, X0 + SIDE)
    ys = slice(Y0, Y0 + deep_y) if dy < 0 else slice(Y0 + SIDE - deep_y, Y0 + SIDE)
    return xs if dx else slice(X0, X0 + SIDE), ys if dy else slice(Y0, Y0 + SIDE)


def moved(box, dx, dy):
    xs, ys = box
    return (
        slice(xs.start - SIDE * dx, xs.stop - SIDE * dx),
        slice(ys.start - SIDE * dy, ys.stop - SIDE * dy),
    )


def wind_groups(dx, dy):
    ys = slice(Y0, Y0 + SIDE) if dy == 0 else slice(Y0 + 8, Y0 + 16) if dy > 0 else slice(Y0, Y0 + 8)
    if dx == 0:
        return [(g, slice(X0 + 4 * g, X0 + 4 * g + 4), ys) for g in range(4)]
    base = X0 + 8 if dx > 0 else X0
    if dy:
        quarters = (2, 3) if dx > 0 else (0, 1)
    else:
        quarters = (1, 2, 3) if dx > 0 else (0, 1, 2)
    return [(g, slice(base + 2 * g, base + 2 * g + 2), ys) for g in quarters]


def local_tendency(src, east, north, flux, xs, ys):
    nx, ny = xs.stop - xs.start, ys.stop - ys.start

    def face_flux(speed, before, center, after, beyond):
        both = 2.0 * (center + after)
        up = jnp.maximum(speed, 0.0)
        down = jnp.minimum(speed, 0.0)
        return up * (both + 3.0 * center - before) + down * (both + 3.0 * after - beyond)

    along_x = src[xs.start - 2 : xs.stop + 2, ys, :]
    flux_x = face_flux(
        east[xs.start - 1 : xs.stop, ys, :],
        along_x[0 : nx + 1],
        along_x[1 : nx + 2],
        along_x[2 : nx + 3],
        along_x[3 : nx + 4],
    )
    total = flux_x[:nx] - flux_x[1:]
    faces = slice(ys.start - 1, ys.stop)
    flux[0:nx, 0 : ny + 1, :] = face_flux(
        north[xs, faces, :],
        src[xs, faces.start - 1 : faces.stop - 1, :],
        src[xs, faces, :],
        src[xs, faces.start + 1 : faces.stop + 1, :],
        src[xs, faces.start + 2 : faces.stop + 2, :],
    )
    return total + (flux[0:nx, 0:ny, :] - flux[0:nx, 1 : ny + 1, :])


def kernel(
    state_ref, wind_ref, regime_ref, lift_ref, output_ref, taps_ref, out_ref,
    state_in, wind_in, regime_in, lift_in, output_in, taps_in,
    field, first, second, east, north, flux, stage,
    send_x, recv_x, send_y, recv_y, send_c, recv_c,
    conv_0, conv_1, conv_2, conv_3, small, lift_map, out_map, spread, pick, unpick, ordered, answers,
    load_sem, halo_send, halo_recv, weight_send, weight_recv, small_send, small_recv,
):
    count_tile, count_sect, count_emu = (lax.axis_size(n) for n in ("tile", "sect", "emu"))
    tile, sect, emu = (lax.axis_index(n) for n in ("tile", "sect", "emu"))
    along_y = sect * count_emu + emu
    total_y = count_sect * count_emu

    def neighbour(dx, dy):
        y = lax.rem(along_y + (dy + total_y), total_y)
        return (lax.rem(tile + (dx + count_tile), count_tile), y // count_emu, lax.rem(y, count_emu))

    half = count_tile // 2
    far_tile = lax.rem(tile + half, count_tile)
    core, chip = lax.rem(sect, 2), sect // 2
    partners = (
        (tile, chip * 2 + (1 - core), emu),
        (tile, (1 - chip) * 2 + core, emu),
        (far_tile, (1 - chip) * 2 + (1 - core), emu),
    )
    neighbours = [neighbour(dx, dy) for dx, dy in DIRECTIONS]

    conv = (conv_0, conv_1, conv_2, conv_3)
    barrier = pltpu.get_barrier_semaphore()
    for device in (*neighbours, *partners):
        pl.semaphore_signal(barrier, inc=1, device_id=device, device_id_type=MESH)

    loads = [
        pltpu.make_async_copy(src, dst, load_sem.at[i])
        for i, (src, dst) in enumerate(
            (
                (wind_ref, wind_in),
                (state_ref, state_in),
                (taps_ref, taps_in),
                (regime_ref, regime_in),
                (lift_ref, lift_in),
                (output_ref, output_in),
            )
        )
    ]
    for copy in loads:
        copy.start()

    row, column = iota((LANES, 8 * LANES), 0), iota((LANES, 8 * LANES), 1)
    group, part = column // (2 * LANES), (column // LANES) % 2
    chosen = (row // LEVELS == part * 4 + group) & (row % LEVELS == column % LEVELS)
    spread[...] = jnp.where(chosen, 1.0, 0.0).astype(BF16)
    loads[0].wait()
    packed = []
    for j in range(4):
        rows = [
            wind_in[pl.ds(c * LEVELS * SIDE + 4 * g + j, LEVELS, stride=SIDE), :]
            for c in range(2)
            for g in range(4)
        ]
        packed.append(jnp.concatenate(rows, axis=0).T)
    wide = dot(jnp.concatenate(packed, axis=0).astype(BF16), spread[...])
    for g in range(4):
        at = (slice(X0 + 4 * g, X0 + 4 * g + 4), slice(Y0, Y0 + SIDE), slice(None))
        east[at] = wide[:, 256 * g : 256 * g + 128].reshape(4, SIDE, LANES)
        north[at] = wide[:, 256 * g + 128 : 256 * g + 256].reshape(4, SIDE, LANES)
    loads[1].wait()
    for x in range(SIDE):
        field[X0 + x, Y0 : Y0 + SIDE, :] = state_in[pl.ds(x, LANES, stride=SIDE), :].T

    def buffers(step, k):
        dx, dy = DIRECTIONS[k]
        if dy == 0:
            return send_x.at[step, k - 4], recv_x.at[step, k - 4]
        if dx == 0:
            return send_y.at[step, k - 6], recv_y.at[step, k - 6]
        return send_c.at[step, k], recv_c.at[step, k]

    def halo_copy(step, k):
        sent, received = buffers(step, k)
        rows = field_rows(*DIRECTIONS[k]) + (wind_rows(*DIRECTIONS[k]) if step == 0 else 0)
        return pltpu.make_async_remote_copy(
            src_ref=sent.at[0:rows],
            dst_ref=received.at[0:rows],
            send_sem=halo_send.at[step, k],
            recv_sem=halo_recv.at[step, k],
            device_id=neighbours[k],
            device_id_type=MESH,
        )

    def pack(step):
        for k, (dx, dy) in enumerate(DIRECTIONS):
            sent, _ = buffers(step, k)
            xs, ys = sent_box(dx, dy)
            rows = field_rows(dx, dy)
            if dx and dy:
                for i in range(CORNER):
                    stage[k, CORNER * i : CORNER * (i + 1), :] = field[xs.start + i, ys, :]
                sent[0:rows, :] = stage[k].astype(BF16)
            else:
                sent[0:rows, :] = field[xs, ys, :].reshape(rows, LANES).astype(BF16)
            if step == 0:
                more = wind_rows(dx, dy)
                quarter = iota((more, LANES), 1) // LEVELS
                packed = jnp.zeros((more, LANES), F32)
                for c, winds in enumerate((east, north)):
                    for g, gx, gy in wind_groups(dx, dy):
                        piece = winds[gx, gy, :].reshape(more, LANES)
                        packed = jnp.where(quarter == c * 4 + g, piece, packed)
                sent[rows : rows + more, :] = packed.astype(BF16)

    def unpack(step):
        for k, (dx, dy) in enumerate(DIRECTIONS):
            _, received = buffers(step, k)
            xs, ys = moved(sent_box(dx, dy), dx, dy)
            rows = field_rows(dx, dy)
            nx, ny = xs.stop - xs.start, ys.stop - ys.start
            if dx and dy:
                stage[k] = received[0:rows, :].astype(F32)
                for i in range(CORNER):
                    field[xs.start + i, ys, :] = stage[k, CORNER * i : CORNER * (i + 1), :]
            else:
                field[xs, ys, :] = received[0:rows, :].astype(F32).reshape(nx, ny, LANES)
            if step == 0:
                more = wind_rows(dx, dy)
                wide = dot(received[rows : rows + more, :], spread[...])
                for g, gx, gy in wind_groups(dx, dy):
                    xs, ys = moved((gx, gy), dx, dy)
                    shape = (xs.stop - xs.start, ys.stop - ys.start, LANES)
                    east[xs, ys, :] = wide[:, 256 * g : 256 * g + 128].reshape(shape)
                    north[xs, ys, :] = wide[:, 256 * g + 128 : 256 * g + 256].reshape(shape)

    pack(0)
    pl.semaphore_wait(barrier, len(neighbours) + len(partners))
    halo = [halo_copy(0, k) for k in range(8)]
    for copy in halo:
        copy.start()

    for copy in loads[2:]:
        copy.wait()
    for layer in range(LAYERS):
        conv[layer][sect] = 0.5 * taps_in[3 * layer : 3 * layer + 3]
    small[sect] = jnp.concatenate([lift_in[...], output_in[...]], axis=0)

    def weight_copies(j):
        copies = [
            pltpu.make_async_remote_copy(
                src_ref=small.at[sect],
                dst_ref=small.at[sect],
                send_sem=small_send.at[j],
                recv_sem=small_recv.at[j],
                device_id=partners[j],
                device_id_type=MESH,
            )
        ]
        for layer in range(LAYERS):
            copies.append(
                pltpu.make_async_remote_copy(
                    src_ref=conv[layer].at[sect],
                    dst_ref=conv[layer].at[sect],
                    send_sem=weight_send.at[j, layer],
                    recv_sem=weight_recv.at[j, layer],
                    device_id=partners[j],
                    device_id_type=MESH,
                )
            )
        return copies

    weights = [weight_copies(j) for j in range(3)]
    for i in range(LAYERS + 1):
        for j in range(3):
            weights[j][i].start()

    regimes = regime_in[...]
    member = jnp.where(regimes == iota((8, 256), 0), 1.0, 0.0)
    earlier = jnp.where(iota((256, 256), 0) < iota((256, 256), 1), 1.0, 0.0).astype(BF16)
    place = member * dot(member.astype(BF16), earlier)
    tiles = jnp.floor((jnp.sum(member, axis=1, keepdims=True) + (TILE - 1)) * (1.0 / TILE))
    before = jnp.where(iota((8, 8), 1) < iota((8, 8), 0), 1.0, 0.0).astype(BF16)
    starts = dot(before, jnp.broadcast_to(tiles, (8, LANES)).astype(BF16))[:, 0:1]
    start = member * starts
    slot_row = jnp.sum(place + TILE * start, axis=0, keepdims=True)
    same = jnp.where(iota((256, 256), 0) == iota((256, 256), 1), 1.0, 0.0).astype(BF16)
    slot_column = jnp.sum(
        dot_nt(same, place.astype(BF16)) + TILE * dot_nt(same, start.astype(BF16)),
        axis=1,
        keepdims=True,
    )
    unpick[...] = jnp.where(
        slot_column == iota((256, PAD_SLOTS), 1).astype(F32), 1.0, 0.0
    ).astype(BF16)
    pick[...] = jnp.where(
        slot_row == iota((SLOTS, 256), 0).astype(F32), 1.0, 0.0
    ).astype(BF16)
    answers[SLOTS:, :] = jnp.zeros((PAD_SLOTS - SLOTS, LANES), BF16)
    tile_regimes = [0] * TILES
    used = 0
    for r in range(REGIMES - 1):
        named = jnp.sum(jnp.where(regimes == r, 1, 0))
        used = used + (named + (TILE - 1)) // TILE
        tile_regimes = [r_of + jnp.where(t >= used, 1, 0) for t, r_of in enumerate(tile_regimes)]

    level_of = iota((TILE, LANES), 1) % LEVELS
    square = jnp.zeros((LANES, LANES), BF16)

    def beside(a, b):
        return jnp.concatenate([a, b], axis=1)

    def over(a, b):
        return jnp.concatenate([a, b], axis=0)

    zero = jnp.zeros((TILE, LANES), BF16)

    def in_pairs(levels):
        return jnp.concatenate([beside(levels[m], levels[m + 1]) for m in range(0, LEVELS, 2)], axis=0)

    def out_of_pairs(rows):
        return [
            rows[m // 2 * TILE : (m // 2 + 1) * TILE, m % 2 * LANES : (m % 2 + 1) * LANES]
            for m in range(LEVELS)
        ]

    def both(tap):
        return over(beside(tap, square), beside(square, tap))

    def lifted(t):
        columns = ordered[t * TILE : (t + 1) * TILE, :]
        masked = [jnp.where(level_of == m, columns, zero) for m in range(LEVELS)]
        return out_of_pairs(dot(in_pairs(masked), both(lift_map[tile_regimes[t]])))

    def layered(t, layer, halves):
        spacing = 2**layer
        below, centre, above = (conv[layer][tile_regimes[t], i] for i in range(3))
        active = []
        for half in halves:
            u = half.astype(BF16)
            active.append(u + u * jnp.tanh(u))
        low = [m for m in range(LEVELS) if m // spacing % 2 == 0]
        pieces = [[active[m] for m in low], [active[m + spacing] for m in low]]
        taps = over(beside(centre, above), beside(below, centre))
        if 2 * spacing < LEVELS:
            pieces.append([active[m - spacing] if m >= spacing else zero for m in low])
            pieces.append(
                [active[m + 2 * spacing] if m + 2 * spacing < LEVELS else zero for m in low]
            )
            taps = beside(taps, over(beside(below, square), beside(square, above)))
        result = dot_nt(
            jnp.concatenate([jnp.concatenate(piece, axis=0) for piece in pieces], axis=1), taps
        )
        halves = list(halves)
        for p, m in enumerate(low):
            rows = slice(p * TILE, (p + 1) * TILE)
            halves[m] = halves[m] + result[rows, :LANES]
            halves[m + spacing] = halves[m + spacing] + result[rows, LANES:]
        return halves

    def answered(t, halves):
        rows = in_pairs([half.astype(BF16) for half in halves])
        pieces = out_of_pairs(dot_nt(rows, both(out_map[tile_regimes[t]])))
        answer = jnp.zeros((TILE, LANES), F32)
        for m in range(LEVELS):
            answer = jnp.where(level_of == m, pieces[m], answer)
        return answer.astype(BF16)

    def network(first_time):
        tiles = [lifted(t) for t in range(TILES)]
        for layer in range(LAYERS):
            if first_time:
                for j in range(3):
                    weights[j][1 + layer].wait_recv()
            tiles = [layered(t, layer, tiles[t]) for t in range(TILES)]
        results = [answered(t, tiles[t]) for t in range(TILES)]
        for t in range(TILES):
            answers[t * TILE : (t + 1) * TILE, :] = results[t]

    own = (slice(X0, X0 + SIDE), slice(Y0, Y0 + SIDE), slice(None))
    for step in range(STEPS):
        if step:
            pack(step)
            halo = [halo_copy(step, k) for k in range(8)]
            for copy in halo:
                copy.start()
        for copy in halo:
            copy.wait_recv()
        unpack(step)
        xs, ys = slice(X0 - 4, X0 + SIDE + 4), slice(Y0 - 4, Y0 + SIDE + 4)
        first[xs, ys, :] = field[xs, ys, :] + (1.0 / 6.0) * local_tendency(
            field, east, north, flux, xs, ys
        )
        xs, ys = slice(X0 - 2, X0 + SIDE + 2), slice(Y0 - 2, Y0 + SIDE + 2)
        second[xs, ys, :] = (
            0.75 * field[xs, ys, :]
            + 0.25 * first[xs, ys, :]
            + (0.25 / 6.0) * local_tendency(first, east, north, flux, xs, ys)
        )
        xs, ys = own[0], own[1]
        dyn = (
            (1.0 / 3.0) * field[own]
            + (2.0 / 3.0) * second[own]
            + (1.0 / 9.0) * local_tendency(second, east, north, flux, xs, ys)
        ).reshape(SIDE * SIDE, LANES)
        ordered[...] = dot(pick[...], dyn.astype(BF16)).astype(BF16)
        if step == 0:
            for j in range(3):
                weights[j][0].wait_recv()
            row, column = iota((LANES, 16), 0), iota((LANES, 16), 1)
            to_lift = jnp.where(row // LEVELS == column, 0.5, 0.0).astype(BF16)
            to_out = jnp.where(row // LEVELS + VARS == column, 2.0, 0.0).astype(BF16)
            for r in range(REGIMES):
                lift_map[r] = dot(to_lift, small[r]).astype(BF16)
                out_map[r] = dot(to_out, small[r]).astype(BF16)
        network(step == 0)
        final = dyn + dot(unpick[...], answers[...])
        if step == STEPS - 1:
            out_ref[...] = final
        else:
            field[own] = final.reshape(SIDE, SIDE, LANES)
        for copy in halo:
            copy.wait_send()
    for j in range(3):
        for copy in weights[j]:
            copy.wait_send()


def per_device(state, winds, regime_table, emu_lift, emu_conv, emu_output):
    cells = SIDE * SIDE
    padded = pltpu.VMEM((PAD_X, PAD_Y, LANES), F32)
    dma = pltpu.SemaphoreType.DMA
    result = pl.pallas_call(
        kernel,
        out_shape=jax.ShapeDtypeStruct((cells, LANES), F32),
        in_specs=[pl.BlockSpec(memory_space=pl.ANY)] * 6,
        out_specs=pl.BlockSpec(memory_space=pltpu.VMEM),
        scratch_shapes=[
            pltpu.VMEM((LANES * SIDE, SIDE), F32),
            pltpu.VMEM((2 * LEVELS * SIDE, SIDE), F32),
            pltpu.VMEM((1, cells), jnp.int32),
            pltpu.VMEM((VARS, LANES), BF16),
            pltpu.VMEM((VARS, LANES), BF16),
            pltpu.VMEM((3 * LAYERS, LANES, LANES), BF16),
            padded, padded, padded, padded, padded,
            pltpu.VMEM((24, PAD_Y, LANES), F32),
            pltpu.VMEM((4, CORNER * CORNER, LANES), F32),
            pltpu.VMEM((STEPS, 2, 128, LANES), BF16),
            pltpu.VMEM((STEPS, 2, 128, LANES), BF16),
            pltpu.VMEM((STEPS, 2, 160, LANES), BF16),
            pltpu.VMEM((STEPS, 2, 160, LANES), BF16),
            pltpu.VMEM((STEPS, 4, 32, LANES), BF16),
            pltpu.VMEM((STEPS, 4, 32, LANES), BF16),
            *[pltpu.VMEM((REGIMES, 3, LANES, LANES), BF16)] * LAYERS,
            pltpu.VMEM((REGIMES, 2 * VARS, LANES), BF16),
            pltpu.VMEM((REGIMES, LANES, LANES), BF16),
            pltpu.VMEM((REGIMES, LANES, LANES), BF16),
            pltpu.VMEM((LANES, 8 * LANES), BF16),
            pltpu.VMEM((SLOTS, cells), BF16),
            pltpu.VMEM((cells, PAD_SLOTS), BF16),
            pltpu.VMEM((SLOTS, LANES), BF16),
            pltpu.VMEM((PAD_SLOTS, LANES), BF16),
            dma((6,)),
            dma((STEPS, 8)), dma((STEPS, 8)),
            dma((3, LAYERS)), dma((3, LAYERS)),
            dma((3,)), dma((3,)),
        ],
        compiler_params=pltpu.CompilerParams(
            collective_id=0, has_side_effects=True, vmem_limit_bytes=60 * 2**20
        ),
    )(
        state.reshape(LANES * SIDE, SIDE),
        winds.reshape(2 * LEVELS * SIDE, SIDE),
        regime_table.reshape(1, cells),
        emu_lift[0].T,
        emu_output[0],
        emu_conv.reshape(3 * LAYERS, LANES, LANES),
    )
    return result.reshape(SIDE, SIDE, VARS, LEVELS).transpose(2, 3, 0, 1)


def solution(mesh):
    in_specs = (
        P(None, None, "tile", ("sect", "emu")),
        P(None, None, "tile", ("sect", "emu")),
        P("tile", ("sect", "emu"), None, None),
        P("sect", None, None),
        P("sect", None, None, None, None),
        P("sect", None, None),
    )
    out_specs = P(None, None, "tile", ("sect", "emu"))
    return jax.shard_map(
        per_device, mesh=mesh, in_specs=in_specs, out_specs=out_specs, check_vma=False
    )
```

```python
import functools

import jax
import jax.numpy as jnp
from jax import lax
from jax.experimental import pallas as pl
from jax.experimental.pallas import tpu as pltpu
from jax.sharding import PartitionSpec as P

MESH = pl.DeviceIdType.MESH
STEPS = 2
SIDE = 16
LANES = 128
VARS = 8
LEVELS = 16
REGIMES = 4
LAYERS = 4
TILE = 32
LATE = 6
SAFE = SIDE - LATE
SAFE_TILES, LATE_TILES = 8, 6
TILES = SAFE_TILES + LATE_TILES
SAFE_SLOTS = SAFE_TILES * TILE
SLOTS = TILES * TILE
PAD_SLOTS = 512
CORNER = 4
X0, Y0 = 8, 8
PAD_X, PAD_Y = 32, 32
DIRECTIONS = ((1, 1), (1, -1), (-1, 1), (-1, -1), (1, 0), (-1, 0), (0, 1), (0, -1))
BF16 = jnp.bfloat16
F32 = jnp.float32


def dot(a, b):
    return jnp.dot(a, b, preferred_element_type=F32)


def dot_nt(a, b):
    return lax.dot_general(a, b, (((1,), (1,)), ((), ())), preferred_element_type=F32)


def iota(shape, dim):
    return lax.broadcasted_iota(jnp.int32, shape, dim)


def field_rows(dx, dy):
    return 96 if dy == 0 else 128 if dx == 0 else CORNER * CORNER


def wind_rows(dx, dy):
    return 16 if dx and dy else 32


def sent_box(dx, dy):
    deep_x, deep_y = (CORNER, CORNER) if dx and dy else (6, 8)
    xs = slice(X0, X0 + deep_x) if dx < 0 else slice(X0 + SIDE - deep_x, X0 + SIDE)
    ys = slice(Y0, Y0 + deep_y) if dy < 0 else slice(Y0 + SIDE - deep_y, Y0 + SIDE)
    return xs if dx else slice(X0, X0 + SIDE), ys if dy else slice(Y0, Y0 + SIDE)


def wind_groups(dx, dy):
    ys = slice(Y0, Y0 + SIDE) if dy == 0 else slice(Y0 + 8, Y0 + 16) if dy > 0 else slice(Y0, Y0 + 8)
    if dx == 0:
        return [(slice(X0 + 4 * g, X0 + 4 * g + 4), ys) for g in range(4)]
    base = X0 + 8 if dx > 0 else X0
    return [(slice(base + 2 * g, base + 2 * g + 2), ys) for g in range(4)]


def local_tendency(src, east, north, flux, x_from, nx, ys):
    ny = ys.stop - ys.start

    def face_flux(speed, before, center, after, beyond):
        both = 2.0 * (center + after)
        up = jnp.maximum(speed, 0.0)
        down = jnp.minimum(speed, 0.0)
        return up * (both + 3.0 * center - before) + down * (both + 3.0 * after - beyond)

    along_x = src[pl.ds(x_from - 2, nx + 4), ys, :]
    flux_x = face_flux(
        east[pl.ds(x_from - 1, nx + 1), ys, :],
        along_x[0 : nx + 1],
        along_x[1 : nx + 2],
        along_x[2 : nx + 3],
        along_x[3 : nx + 4],
    )
    total = flux_x[:nx] - flux_x[1:]
    xs = pl.ds(x_from, nx)
    start, stop = ys.start - 1, ys.stop
    flux[0:nx, 0 : ny + 1, :] = face_flux(
        north[xs, start:stop, :],
        src[xs, start - 1 : stop - 1, :],
        src[xs, start:stop, :],
        src[xs, start + 1 : stop + 1, :],
        src[xs, start + 2 : stop + 2, :],
    )
    return total + (flux[0:nx, 0:ny, :] - flux[0:nx, 1 : ny + 1, :])


def kernel(
    state_ref, wind_ref, regime_ref, lift_ref, output_ref, taps_ref, out_ref,
    state_in, wind_in, regime_in, lift_in, output_in, taps_in,
    field, first, second, east, north, flux, stage,
    send_x, recv_x, send_y, recv_y, send_c, recv_c,
    conv_0, conv_1, conv_2, conv_3, small, lift_map, out_map, spread, pick, unpick, ordered, answers, dyn,
    load_sem, halo_send, halo_recv, weight_send, weight_recv, small_send, small_recv,
):
    count_tile, count_sect, count_emu = (lax.axis_size(n) for n in ("tile", "sect", "emu"))
    tile, sect, emu = (lax.axis_index(n) for n in ("tile", "sect", "emu"))
    along_y = sect * count_emu + emu
    total_y = count_sect * count_emu

    def neighbour(dx, dy):
        y = lax.rem(along_y + (dy + total_y), total_y)
        return (lax.rem(tile + (dx + count_tile), count_tile), y // count_emu, lax.rem(y, count_emu))

    half = count_tile // 2
    upper = lax.rem(tile, half) // (half // 2)
    safe_from, late_from = LATE * (1 - upper), SAFE * upper
    far_tile = lax.rem(tile + half, count_tile)
    core, chip = lax.rem(sect, 2), sect // 2
    partners = (
        (tile, chip * 2 + (1 - core), emu),
        (tile, (1 - chip) * 2 + core, emu),
        (far_tile, (1 - chip) * 2 + (1 - core), emu),
    )
    neighbours = [neighbour(dx, dy) for dx, dy in DIRECTIONS]

    conv = (conv_0, conv_1, conv_2, conv_3)
    barrier = pltpu.get_barrier_semaphore()
    for device in (*neighbours, *partners):
        pl.semaphore_signal(barrier, inc=1, device_id=device, device_id_type=MESH)

    loads = [
        pltpu.make_async_copy(src, dst, load_sem.at[i])
        for i, (src, dst) in enumerate(
            (
                (wind_ref, wind_in),
                (state_ref, state_in),
                (taps_ref, taps_in),
                (regime_ref, regime_in),
                (lift_ref, lift_in),
                (output_ref, output_in),
            )
        )
    ]
    for copy in loads:
        copy.start()

    row, column = iota((LANES, 8 * LANES), 0), iota((LANES, 8 * LANES), 1)
    group, part = column // (2 * LANES), (column // LANES) % 2
    chosen = (row // LEVELS == part * 4 + group) & (row % LEVELS == column % LEVELS)
    spread[...] = jnp.where(chosen, 1.0, 0.0).astype(BF16)
    loads[0].wait()
    packed = []
    for j in range(4):
        rows = [
            wind_in[pl.ds(c * LEVELS * SIDE + 4 * g + j, LEVELS, stride=SIDE), :]
            for c in range(2)
            for g in range(4)
        ]
        packed.append(jnp.concatenate(rows, axis=0).T)
    wide = dot(jnp.concatenate(packed, axis=0).astype(BF16), spread[...])
    for g in range(4):
        at = (slice(X0 + 4 * g, X0 + 4 * g + 4), slice(Y0, Y0 + SIDE), slice(None))
        east[at] = wide[:, 256 * g : 256 * g + 128].reshape(4, SIDE, LANES)
        north[at] = wide[:, 256 * g + 128 : 256 * g + 256].reshape(4, SIDE, LANES)
    loads[1].wait()
    for x in range(SIDE):
        field[X0 + x, Y0 : Y0 + SIDE, :] = state_in[pl.ds(x, LANES, stride=SIDE), :].T

    def buffers(step, k):
        dx, dy = DIRECTIONS[k]
        if dy == 0:
            return send_x.at[step, k - 4], recv_x.at[step, k - 4]
        if dx == 0:
            return send_y.at[step, k - 6], recv_y.at[step, k - 6]
        return send_c.at[step, k], recv_c.at[step, k]

    def halo_copy(step, k):
        sent, received = buffers(step, k)
        rows = field_rows(*DIRECTIONS[k]) + (wind_rows(*DIRECTIONS[k]) if step == 0 else 0)
        return pltpu.make_async_remote_copy(
            src_ref=sent.at[0:rows],
            dst_ref=received.at[0:rows],
            send_sem=halo_send.at[step, k],
            recv_sem=halo_recv.at[step, k],
            device_id=neighbours[k],
            device_id_type=MESH,
        )

    def pack(step):
        for k, (dx, dy) in enumerate(DIRECTIONS):
            sent, _ = buffers(step, k)
            xs, ys = sent_box(dx, dy)
            rows = field_rows(dx, dy)
            if dx and dy:
                for i in range(CORNER):
                    stage[k, CORNER * i : CORNER * (i + 1), :] = field[xs.start + i, ys, :]
                sent[0:rows, :] = stage[k].astype(BF16)
            else:
                sent[0:rows, :] = field[xs, ys, :].reshape(rows, LANES).astype(BF16)
            if step == 0:
                more = wind_rows(dx, dy)
                quarter = iota((more, LANES), 1) // LEVELS
                packed = jnp.zeros((more, LANES), F32)
                for c, winds in enumerate((east, north)):
                    for g, (gx, gy) in enumerate(wind_groups(dx, dy)):
                        piece = winds[gx, gy, :].reshape(more, LANES)
                        packed = jnp.where(quarter == c * 4 + g, piece, packed)
                sent[rows : rows + more, :] = packed.astype(BF16)

    def arrive(step, k, ref, rows):
        pltpu.make_async_remote_copy(
            src_ref=ref.at[0:rows],
            dst_ref=ref.at[0:rows],
            send_sem=halo_send.at[step, k],
            recv_sem=halo_recv.at[step, k],
            device_id=neighbours[0],
            device_id_type=MESH,
        ).wait_recv()

    def unpack_winds(packed, x_from, ys):
        wide = dot(packed, spread[...])
        ny = ys.stop - ys.start
        deep = packed.shape[0] // ny
        for g in range(4):
            xs = pl.ds(x_from + deep * g, deep)
            east[xs, ys, :] = wide[:, 256 * g : 256 * g + 128].reshape(deep, ny, LANES)
            north[xs, ys, :] = wide[:, 256 * g + 128 : 256 * g + 256].reshape(deep, ny, LANES)

    def receive_y(step):
        for k, ys in ((6, slice(Y0 - 8, Y0)), (7, slice(Y0 + SIDE, Y0 + SIDE + 8))):
            rows, more = 128, 32 if step == 0 else 0
            ref = recv_y.at[step, k - 6]
            arrive(step, k, ref, rows + more)
            field[X0 : X0 + SIDE, ys, :] = ref[0:rows, :].astype(F32).reshape(SIDE, 8, LANES)
            if step == 0:
                unpack_winds(ref[rows : rows + more, :], X0, ys)

    def receive_x(step, side):
        rows, more = 96, 32 if step == 0 else 0
        ref = recv_x.at[step, side]
        arrive(step, 4 + side, ref, rows + more)
        own_y = slice(Y0, Y0 + SIDE)
        xs = pl.ds(X0 - 6 + (SIDE + 6) * side, 6)
        field[xs, own_y, :] = ref[0:rows, :].astype(F32).reshape(6, SIDE, LANES)
        winds_from = X0 - 8 + (SIDE + 8) * side
        if step == 0:
            unpack_winds(ref[rows : rows + more, :], winds_from, own_y)
        x_from = X0 - CORNER + (SIDE + CORNER) * side
        for j, start, wide_start in ((0, Y0 - CORNER, Y0 - 8), (1, Y0 + SIDE, Y0 + SIDE)):
            rows, more = CORNER * CORNER, 16 if step == 0 else 0
            ref = recv_c.at[step, 2 * side + j]
            arrive(step, 2 * side + j, ref, rows + more)
            stage[j] = ref[0:rows, :].astype(F32)
            for i in range(CORNER):
                field[x_from + i, start : start + CORNER, :] = stage[j, CORNER * i : CORNER * (i + 1), :]
            if step == 0:
                unpack_winds(ref[rows : rows + more, :], winds_from, slice(wide_start, wide_start + 8))

    pack(0)
    pl.semaphore_wait(barrier, len(neighbours) + len(partners))
    halo = [halo_copy(0, k) for k in range(8)]
    for copy in halo:
        copy.start()

    for copy in loads[2:]:
        copy.wait()
    for layer in range(LAYERS):
        conv[layer][sect] = 0.5 * taps_in[3 * layer : 3 * layer + 3]
    small[sect] = jnp.concatenate([lift_in[...], output_in[...]], axis=0)

    def weight_copies(j):
        copies = [
            pltpu.make_async_remote_copy(
                src_ref=small.at[sect],
                dst_ref=small.at[sect],
                send_sem=small_send.at[j],
                recv_sem=small_recv.at[j],
                device_id=partners[j],
                device_id_type=MESH,
            )
        ]
        for layer in range(LAYERS):
            copies.append(
                pltpu.make_async_remote_copy(
                    src_ref=conv[layer].at[sect],
                    dst_ref=conv[layer].at[sect],
                    send_sem=weight_send.at[j, layer],
                    recv_sem=weight_recv.at[j, layer],
                    device_id=partners[j],
                    device_id_type=MESH,
                )
            )
        return copies

    weights = [weight_copies(j) for j in range(3)]
    for i in range(LAYERS + 1):
        for j in range(3):
            weights[j][i].start()

    row_of = iota((1, 256), 1) // SIDE
    late = jnp.where((row_of >= late_from) & (row_of < late_from + LATE), 1, 0)
    groups = regime_in[...] + REGIMES * late
    member = jnp.where(groups == iota((8, 256), 0), 1.0, 0.0)
    earlier = jnp.where(iota((256, 256), 0) < iota((256, 256), 1), 1.0, 0.0).astype(BF16)
    place = member * dot(member.astype(BF16), earlier)
    tiles = jnp.floor((jnp.sum(member, axis=1, keepdims=True) + (TILE - 1)) * (1.0 / TILE))
    one, other = iota((8, 8), 0), iota((8, 8), 1)
    before = jnp.where((other < one) & (other // REGIMES == one // REGIMES), 1.0, 0.0).astype(BF16)
    starts = dot(before, jnp.broadcast_to(tiles, (8, LANES)).astype(BF16))[:, 0:1]
    starts = starts + jnp.where(iota((8, 1), 0) >= REGIMES, float(SAFE_TILES), 0.0)
    start = member * starts
    slot_row = jnp.sum(place + TILE * start, axis=0, keepdims=True)
    same = jnp.where(iota((256, 256), 0) == iota((256, 256), 1), 1.0, 0.0).astype(BF16)
    slot_column = jnp.sum(
        dot_nt(same, place.astype(BF16)) + TILE * dot_nt(same, start.astype(BF16)),
        axis=1,
        keepdims=True,
    )
    unpick[...] = jnp.where(
        slot_column == iota((256, PAD_SLOTS), 1).astype(F32), 1.0, 0.0
    ).astype(BF16)
    pick[...] = jnp.where(
        slot_row == iota((SLOTS, 256), 0).astype(F32), 1.0, 0.0
    ).astype(BF16)
    answers[SLOTS:, :] = jnp.zeros((PAD_SLOTS - SLOTS, LANES), BF16)
    dyn[...] = jnp.zeros((SIDE * SIDE, LANES), F32)
    tile_regimes = []
    for part, count in enumerate((SAFE_TILES, LATE_TILES)):
        numbers = [0] * count
        used = 0
        for r in range(REGIMES - 1):
            named = jnp.sum(jnp.where(groups == REGIMES * part + r, 1, 0))
            used = used + (named + (TILE - 1)) // TILE
            numbers = [number + jnp.where(t >= used, 1, 0) for t, number in enumerate(numbers)]
        tile_regimes += numbers

    level_of = iota((TILE, LANES), 1) % LEVELS
    square = jnp.zeros((LANES, LANES), BF16)

    def beside(a, b):
        return jnp.concatenate([a, b], axis=1)

    def over(a, b):
        return jnp.concatenate([a, b], axis=0)

    zero = jnp.zeros((TILE, LANES), BF16)

    def in_pairs(levels):
        return jnp.concatenate([beside(levels[m], levels[m + 1]) for m in range(0, LEVELS, 2)], axis=0)

    def out_of_pairs(rows):
        return [
            rows[m // 2 * TILE : (m // 2 + 1) * TILE, m % 2 * LANES : (m % 2 + 1) * LANES]
            for m in range(LEVELS)
        ]

    def both(tap):
        return over(beside(tap, square), beside(square, tap))

    def lifted(t):
        columns = ordered[t * TILE : (t + 1) * TILE, :]
        masked = [jnp.where(level_of == m, columns, zero) for m in range(LEVELS)]
        return out_of_pairs(dot(in_pairs(masked), both(lift_map[tile_regimes[t]])))

    def layered(t, layer, halves):
        spacing = 2**layer
        below, centre, above = (conv[layer][tile_regimes[t], i] for i in range(3))
        active = []
        for half in halves:
            u = half.astype(BF16)
            active.append(u + u * jnp.tanh(u))
        low = [m for m in range(LEVELS) if m // spacing % 2 == 0]
        pieces = [[active[m] for m in low], [active[m + spacing] for m in low]]
        taps = over(beside(centre, above), beside(below, centre))
        if 2 * spacing < LEVELS:
            pieces.append([active[m - spacing] if m >= spacing else zero for m in low])
            pieces.append(
                [active[m + 2 * spacing] if m + 2 * spacing < LEVELS else zero for m in low]
            )
            taps = beside(taps, over(beside(below, square), beside(square, above)))
        result = dot_nt(
            jnp.concatenate([jnp.concatenate(piece, axis=0) for piece in pieces], axis=1), taps
        )
        halves = list(halves)
        for p, m in enumerate(low):
            rows = slice(p * TILE, (p + 1) * TILE)
            halves[m] = halves[m] + result[rows, :LANES]
            halves[m + spacing] = halves[m + spacing] + result[rows, LANES:]
        return halves

    def answered(t, halves):
        rows = in_pairs([half.astype(BF16) for half in halves])
        pieces = out_of_pairs(dot_nt(rows, both(out_map[tile_regimes[t]])))
        answer = jnp.zeros((TILE, LANES), F32)
        for m in range(LEVELS):
            answer = jnp.where(level_of == m, pieces[m], answer)
        return answer.astype(BF16)

    def network(numbers, first_time):
        tiles = [lifted(t) for t in numbers]
        for layer in range(LAYERS):
            if first_time:
                for j in range(3):
                    weights[j][1 + layer].wait_recv()
            tiles = [layered(t, layer, halves) for t, halves in zip(numbers, tiles)]
        results = [answered(t, halves) for t, halves in zip(numbers, tiles)]
        for t, result in zip(numbers, results):
            answers[t * TILE : (t + 1) * TILE, :] = result

    def advance(x_from, rows, safe):
        more = 2 * (4 if safe else 0)
        ys = slice(Y0 - 4, Y0 + SIDE + 4)
        at = X0 - 4 + x_from if safe else X0 - 4 + (SAFE + 8) * upper
        xs = pl.ds(at, rows + more)
        first[xs, ys, :] = field[xs, ys, :] + (1.0 / 6.0) * local_tendency(
            field, east, north, flux, at, rows + more, ys
        )
        more = 2 * (2 if safe else 0)
        ys = slice(Y0 - 2, Y0 + SIDE + 2)
        at = X0 - 2 + x_from if safe else X0 - 2 + (SAFE + 4) * upper
        xs = pl.ds(at, rows + more)
        second[xs, ys, :] = (
            0.75 * field[xs, ys, :]
            + 0.25 * first[xs, ys, :]
            + (0.25 / 6.0) * local_tendency(first, east, north, flux, at, rows + more, ys)
        )
        ys = slice(Y0, Y0 + SIDE)
        at = X0 + x_from
        xs = pl.ds(at, rows)
        value = (
            (1.0 / 3.0) * field[xs, ys, :]
            + (2.0 / 3.0) * second[xs, ys, :]
            + (1.0 / 9.0) * local_tendency(second, east, north, flux, at, rows, ys)
        )
        cells = pl.ds(pl.multiple_of(x_from * SIDE, SIDE), rows * SIDE)
        dyn[cells, :] = value.reshape(rows * SIDE, LANES)

    def half_step(step, safe):
        x_from, rows = (safe_from, SAFE) if safe else (late_from, LATE)
        numbers = range(SAFE_TILES) if safe else range(SAFE_TILES, TILES)
        slots = slice(0, SAFE_SLOTS) if safe else slice(SAFE_SLOTS, SLOTS)
        read = slice(0, SAFE_SLOTS) if safe else slice(SAFE_SLOTS, PAD_SLOTS)
        advance(x_from, rows, safe)
        ordered[slots, :] = dot(pick[slots, :], dyn[...].astype(BF16)).astype(BF16)
        network(numbers, safe and step == 0)
        cells = pl.ds(pl.multiple_of(x_from * SIDE, SIDE), rows * SIDE)
        final = dyn[cells, :] + dot(unpick[cells, read], answers[read, :])
        if step < STEPS - 1:
            xs = pl.ds(X0 + x_from, rows)
            field[xs, Y0 : Y0 + SIDE, :] = final.reshape(rows, SIDE, LANES)
        else:
            for i in range(rows):
                out_ref[pl.ds(x_from + i, LANES, stride=SIDE), :] = final[SIDE * i : SIDE * (i + 1)].T

    for step in range(STEPS):
        if step:
            pack(step)
            halo = [halo_copy(step, k) for k in range(8)]
            for copy in halo:
                copy.start()
        receive_y(step)
        receive_x(step, 1 - upper)
        if step == 0:
            for j in range(3):
                weights[j][0].wait_recv()
            row, column = iota((LANES, 16), 0), iota((LANES, 16), 1)
            to_lift = jnp.where(row // LEVELS == column, 0.5, 0.0).astype(BF16)
            to_out = jnp.where(row // LEVELS + VARS == column, 2.0, 0.0).astype(BF16)
            for r in range(REGIMES):
                lift_map[r] = dot(to_lift, small[r]).astype(BF16)
                out_map[r] = dot(to_out, small[r]).astype(BF16)
        half_step(step, True)
        receive_x(step, upper)
        half_step(step, False)
        for copy in halo:
            copy.wait_send()
    for j in range(3):
        for copy in weights[j]:
            copy.wait_send()


def per_device(state, winds, regime_table, emu_lift, emu_conv, emu_output):
    cells = SIDE * SIDE
    padded = pltpu.VMEM((PAD_X, PAD_Y, LANES), F32)
    dma = pltpu.SemaphoreType.DMA
    result = pl.pallas_call(
        kernel,
        out_shape=jax.ShapeDtypeStruct((LANES * SIDE, SIDE), F32),
        in_specs=[pl.BlockSpec(memory_space=pl.ANY)] * 6,
        out_specs=pl.BlockSpec(memory_space=pltpu.VMEM),
        scratch_shapes=[
            pltpu.VMEM((LANES * SIDE, SIDE), F32),
            pltpu.VMEM((2 * LEVELS * SIDE, SIDE), F32),
            pltpu.VMEM((1, cells), jnp.int32),
            pltpu.VMEM((VARS, LANES), BF16),
            pltpu.VMEM((VARS, LANES), BF16),
            pltpu.VMEM((3 * LAYERS, LANES, LANES), BF16),
            padded, padded, padded, padded, padded,
            pltpu.VMEM((24, PAD_Y, LANES), F32),
            pltpu.VMEM((4, CORNER * CORNER, LANES), F32),
            pltpu.VMEM((STEPS, 2, 128, LANES), BF16),
            pltpu.VMEM((STEPS, 2, 128, LANES), BF16),
            pltpu.VMEM((STEPS, 2, 160, LANES), BF16),
            pltpu.VMEM((STEPS, 2, 160, LANES), BF16),
            pltpu.VMEM((STEPS, 4, 32, LANES), BF16),
            pltpu.VMEM((STEPS, 4, 32, LANES), BF16),
            *[pltpu.VMEM((REGIMES, 3, LANES, LANES), BF16)] * LAYERS,
            pltpu.VMEM((REGIMES, 2 * VARS, LANES), BF16),
            pltpu.VMEM((REGIMES, LANES, LANES), BF16),
            pltpu.VMEM((REGIMES, LANES, LANES), BF16),
            pltpu.VMEM((LANES, 8 * LANES), BF16),
            pltpu.VMEM((SLOTS, cells), BF16),
            pltpu.VMEM((cells, PAD_SLOTS), BF16),
            pltpu.VMEM((SLOTS, LANES), BF16),
            pltpu.VMEM((PAD_SLOTS, LANES), BF16),
            pltpu.VMEM((cells, LANES), F32),
            dma((6,)),
            dma((STEPS, 8)), dma((STEPS, 8)),
            dma((3, LAYERS)), dma((3, LAYERS)),
            dma((3,)), dma((3,)),
        ],
        compiler_params=pltpu.CompilerParams(
            collective_id=0, has_side_effects=True, vmem_limit_bytes=60 * 2**20
        ),
    )(
        state.reshape(LANES * SIDE, SIDE),
        winds.reshape(2 * LEVELS * SIDE, SIDE),
        regime_table.reshape(1, cells),
        emu_lift[0].T,
        emu_output[0],
        emu_conv.reshape(3 * LAYERS, LANES, LANES),
    )
    return result.reshape(VARS, LEVELS, SIDE, SIDE)


def solution(mesh):
    in_specs = (
        P(None, None, "tile", ("sect", "emu")),
        P(None, None, "tile", ("sect", "emu")),
        P("tile", ("sect", "emu"), None, None),
        P("sect", None, None),
        P("sect", None, None, None, None),
        P("sect", None, None),
    )
    out_specs = P(None, None, "tile", ("sect", "emu"))
    return jax.shard_map(
        per_device, mesh=mesh, in_specs=in_specs, out_specs=out_specs, check_vma=False
    )
```

```python
import functools

import jax
import jax.numpy as jnp
from jax import lax
from jax.experimental import pallas as pl
from jax.experimental.pallas import tpu as pltpu
from jax.sharding import PartitionSpec as P

MESH = pl.DeviceIdType.MESH
STEPS = 2
SIDE = 16
LANES = 128
VARS = 8
LEVELS = 16
REGIMES = 4
LAYERS = 4
TILE = 32
LATE = 6
SAFE = SIDE - LATE
TILES = 11
SLOTS = TILES * TILE
PAD_SLOTS = 384
CORNER = 4
X0, Y0 = 8, 8
PAD_X, PAD_Y = 32, 32
DIRECTIONS = ((1, 1), (1, -1), (-1, 1), (-1, -1), (1, 0), (-1, 0), (0, 1), (0, -1))
BF16 = jnp.bfloat16
F32 = jnp.float32


def dot(a, b):
    return jnp.dot(a, b, preferred_element_type=F32)


def dot_nt(a, b):
    return lax.dot_general(a, b, (((1,), (1,)), ((), ())), preferred_element_type=F32)


def iota(shape, dim):
    return lax.broadcasted_iota(jnp.int32, shape, dim)


def field_rows(dx, dy):
    return 96 if dy == 0 else 128 if dx == 0 else CORNER * CORNER


def wind_rows(dx, dy):
    return 16 if dx and dy else 32


def sent_box(dx, dy):
    deep_x, deep_y = (CORNER, CORNER) if dx and dy else (6, 8)
    xs = slice(X0, X0 + deep_x) if dx < 0 else slice(X0 + SIDE - deep_x, X0 + SIDE)
    ys = slice(Y0, Y0 + deep_y) if dy < 0 else slice(Y0 + SIDE - deep_y, Y0 + SIDE)
    return xs if dx else slice(X0, X0 + SIDE), ys if dy else slice(Y0, Y0 + SIDE)


def wind_groups(dx, dy):
    ys = slice(Y0, Y0 + SIDE) if dy == 0 else slice(Y0 + 8, Y0 + 16) if dy > 0 else slice(Y0, Y0 + 8)
    if dx == 0:
        return [(slice(X0 + 4 * g, X0 + 4 * g + 4), ys) for g in range(4)]
    base = X0 + 8 if dx > 0 else X0
    return [(slice(base + 2 * g, base + 2 * g + 2), ys) for g in range(4)]


def local_tendency(src, east, north, flux, x_from, nx, ys):
    ny = ys.stop - ys.start

    def face_flux(speed, before, center, after, beyond):
        both = 2.0 * (center + after)
        up = jnp.maximum(speed, 0.0)
        down = jnp.minimum(speed, 0.0)
        return up * (both + 3.0 * center - before) + down * (both + 3.0 * after - beyond)

    along_x = src[pl.ds(x_from - 2, nx + 4), ys, :]
    flux_x = face_flux(
        east[pl.ds(x_from - 1, nx + 1), ys, :],
        along_x[0 : nx + 1],
        along_x[1 : nx + 2],
        along_x[2 : nx + 3],
        along_x[3 : nx + 4],
    )
    total = flux_x[:nx] - flux_x[1:]
    xs = pl.ds(x_from, nx)
    start, stop = ys.start - 1, ys.stop
    flux[0:nx, 0 : ny + 1, :] = face_flux(
        north[xs, start:stop, :],
        src[xs, start - 1 : stop - 1, :],
        src[xs, start:stop, :],
        src[xs, start + 1 : stop + 1, :],
        src[xs, start + 2 : stop + 2, :],
    )
    return total + (flux[0:nx, 0:ny, :] - flux[0:nx, 1 : ny + 1, :])


def kernel(
    state_ref, wind_ref, regime_ref, lift_ref, output_ref, taps_ref, out_ref,
    state_in, wind_in, regime_in, lift_in, output_in, taps_in,
    field, first, second, east, north, flux, stage,
    send_x, recv_x, send_y, recv_y, send_c, recv_c,
    conv_0, conv_1, conv_2, conv_3, small, lift_map, out_map, spread, pick, unpick, ordered, answers, dyn,
    load_sem, halo_send, halo_recv, weight_send, weight_recv, small_send, small_recv,
):
    count_tile, count_sect, count_emu = (lax.axis_size(n) for n in ("tile", "sect", "emu"))
    tile, sect, emu = (lax.axis_index(n) for n in ("tile", "sect", "emu"))
    along_y = sect * count_emu + emu
    total_y = count_sect * count_emu

    def neighbour(dx, dy):
        y = lax.rem(along_y + (dy + total_y), total_y)
        return (lax.rem(tile + (dx + count_tile), count_tile), y // count_emu, lax.rem(y, count_emu))

    half = count_tile // 2
    upper = lax.rem(tile, half) // (half // 2)
    safe_from, late_from = LATE * (1 - upper), SAFE * upper
    far_tile = lax.rem(tile + half, count_tile)
    core, chip = lax.rem(sect, 2), sect // 2
    partners = (
        (tile, chip * 2 + (1 - core), emu),
        (tile, (1 - chip) * 2 + core, emu),
        (far_tile, (1 - chip) * 2 + (1 - core), emu),
    )
    neighbours = [neighbour(dx, dy) for dx, dy in DIRECTIONS]

    conv = (conv_0, conv_1, conv_2, conv_3)
    barrier = pltpu.get_barrier_semaphore()
    for device in (*neighbours, *partners):
        pl.semaphore_signal(barrier, inc=1, device_id=device, device_id_type=MESH)

    loads = [
        pltpu.make_async_copy(src, dst, load_sem.at[i])
        for i, (src, dst) in enumerate(
            (
                (wind_ref, wind_in),
                (state_ref, state_in),
                (taps_ref, taps_in),
                (regime_ref, regime_in),
                (lift_ref, lift_in),
                (output_ref, output_in),
            )
        )
    ]
    for copy in loads:
        copy.start()

    row, column = iota((LANES, 8 * LANES), 0), iota((LANES, 8 * LANES), 1)
    group, part = column // (2 * LANES), (column // LANES) % 2
    chosen = (row // LEVELS == part * 4 + group) & (row % LEVELS == column % LEVELS)
    spread[...] = jnp.where(chosen, 1.0, 0.0).astype(BF16)
    loads[0].wait()
    packed = []
    for j in range(4):
        rows = [
            wind_in[pl.ds(c * LEVELS * SIDE + 4 * g + j, LEVELS, stride=SIDE), :]
            for c in range(2)
            for g in range(4)
        ]
        packed.append(jnp.concatenate(rows, axis=0).T)
    wide = dot(jnp.concatenate(packed, axis=0).astype(BF16), spread[...])
    for g in range(4):
        at = (slice(X0 + 4 * g, X0 + 4 * g + 4), slice(Y0, Y0 + SIDE), slice(None))
        east[at] = wide[:, 256 * g : 256 * g + 128].reshape(4, SIDE, LANES)
        north[at] = wide[:, 256 * g + 128 : 256 * g + 256].reshape(4, SIDE, LANES)
    loads[1].wait()
    for x in range(SIDE):
        field[X0 + x, Y0 : Y0 + SIDE, :] = state_in[pl.ds(x, LANES, stride=SIDE), :].T

    def buffers(step, k):
        dx, dy = DIRECTIONS[k]
        if dy == 0:
            return send_x.at[step, k - 4], recv_x.at[step, k - 4]
        if dx == 0:
            return send_y.at[step, k - 6], recv_y.at[step, k - 6]
        return send_c.at[step, k], recv_c.at[step, k]

    def halo_copy(step, k):
        sent, received = buffers(step, k)
        rows = field_rows(*DIRECTIONS[k]) + (wind_rows(*DIRECTIONS[k]) if step == 0 else 0)
        return pltpu.make_async_remote_copy(
            src_ref=sent.at[0:rows],
            dst_ref=received.at[0:rows],
            send_sem=halo_send.at[step, k],
            recv_sem=halo_recv.at[step, k],
            device_id=neighbours[k],
            device_id_type=MESH,
        )

    def pack(step):
        for k, (dx, dy) in enumerate(DIRECTIONS):
            sent, _ = buffers(step, k)
            xs, ys = sent_box(dx, dy)
            rows = field_rows(dx, dy)
            if dx and dy:
                for i in range(CORNER):
                    stage[k, CORNER * i : CORNER * (i + 1), :] = field[xs.start + i, ys, :]
                sent[0:rows, :] = stage[k].astype(BF16)
            else:
                sent[0:rows, :] = field[xs, ys, :].reshape(rows, LANES).astype(BF16)
            if step == 0:
                more = wind_rows(dx, dy)
                quarter = iota((more, LANES), 1) // LEVELS
                packed = jnp.zeros((more, LANES), F32)
                for c, winds in enumerate((east, north)):
                    for g, (gx, gy) in enumerate(wind_groups(dx, dy)):
                        piece = winds[gx, gy, :].reshape(more, LANES)
                        packed = jnp.where(quarter == c * 4 + g, piece, packed)
                sent[rows : rows + more, :] = packed.astype(BF16)

    def arrive(step, k, ref, rows):
        pltpu.make_async_remote_copy(
            src_ref=ref.at[0:rows],
            dst_ref=ref.at[0:rows],
            send_sem=halo_send.at[step, k],
            recv_sem=halo_recv.at[step, k],
            device_id=neighbours[0],
            device_id_type=MESH,
        ).wait_recv()

    def unpack_winds(packed, x_from, ys):
        wide = dot(packed, spread[...])
        ny = ys.stop - ys.start
        deep = packed.shape[0] // ny
        for g in range(4):
            xs = pl.ds(x_from + deep * g, deep)
            east[xs, ys, :] = wide[:, 256 * g : 256 * g + 128].reshape(deep, ny, LANES)
            north[xs, ys, :] = wide[:, 256 * g + 128 : 256 * g + 256].reshape(deep, ny, LANES)

    def receive_y(step):
        for k, ys in ((6, slice(Y0 - 8, Y0)), (7, slice(Y0 + SIDE, Y0 + SIDE + 8))):
            rows, more = 128, 32 if step == 0 else 0
            ref = recv_y.at[step, k - 6]
            arrive(step, k, ref, rows + more)
            field[X0 : X0 + SIDE, ys, :] = ref[0:rows, :].astype(F32).reshape(SIDE, 8, LANES)
            if step == 0:
                unpack_winds(ref[rows : rows + more, :], X0, ys)

    def receive_x(step, side):
        rows, more = 96, 32 if step == 0 else 0
        ref = recv_x.at[step, side]
        arrive(step, 4 + side, ref, rows + more)
        own_y = slice(Y0, Y0 + SIDE)
        xs = pl.ds(X0 - 6 + (SIDE + 6) * side, 6)
        field[xs, own_y, :] = ref[0:rows, :].astype(F32).reshape(6, SIDE, LANES)
        winds_from = X0 - 8 + (SIDE + 8) * side
        if step == 0:
            unpack_winds(ref[rows : rows + more, :], winds_from, own_y)
        x_from = X0 - CORNER + (SIDE + CORNER) * side
        for j, start, wide_start in ((0, Y0 - CORNER, Y0 - 8), (1, Y0 + SIDE, Y0 + SIDE)):
            rows, more = CORNER * CORNER, 16 if step == 0 else 0
            ref = recv_c.at[step, 2 * side + j]
            arrive(step, 2 * side + j, ref, rows + more)
            stage[j] = ref[0:rows, :].astype(F32)
            for i in range(CORNER):
                field[x_from + i, start : start + CORNER, :] = stage[j, CORNER * i : CORNER * (i + 1), :]
            if step == 0:
                unpack_winds(ref[rows : rows + more, :], winds_from, slice(wide_start, wide_start + 8))

    pack(0)
    pl.semaphore_wait(barrier, len(neighbours) + len(partners))
    halo = [halo_copy(0, k) for k in range(8)]
    for copy in halo:
        copy.start()

    for copy in loads[2:]:
        copy.wait()
    for layer in range(LAYERS):
        conv[layer][sect] = 0.5 * taps_in[3 * layer : 3 * layer + 3]
    small[sect] = jnp.concatenate([lift_in[...], output_in[...]], axis=0)

    def weight_copies(j):
        copies = [
            pltpu.make_async_remote_copy(
                src_ref=small.at[sect],
                dst_ref=small.at[sect],
                send_sem=small_send.at[j],
                recv_sem=small_recv.at[j],
                device_id=partners[j],
                device_id_type=MESH,
            )
        ]
        for layer in range(LAYERS):
            copies.append(
                pltpu.make_async_remote_copy(
                    src_ref=conv[layer].at[sect],
                    dst_ref=conv[layer].at[sect],
                    send_sem=weight_send.at[j, layer],
                    recv_sem=weight_recv.at[j, layer],
                    device_id=partners[j],
                    device_id_type=MESH,
                )
            )
        return copies

    weights = [weight_copies(j) for j in range(3)]
    for i in range(LAYERS + 1):
        for j in range(3):
            weights[j][i].start()

    regimes = regime_in[...]
    member = jnp.where(regimes == iota((8, 256), 0), 1.0, 0.0)
    earlier = jnp.where(iota((256, 256), 0) < iota((256, 256), 1), 1.0, 0.0).astype(BF16)
    place = member * dot(member.astype(BF16), earlier)
    tiles = jnp.floor((jnp.sum(member, axis=1, keepdims=True) + (TILE - 1)) * (1.0 / TILE))
    before = jnp.where(iota((8, 8), 1) < iota((8, 8), 0), 1.0, 0.0).astype(BF16)
    starts = dot(before, jnp.broadcast_to(tiles, (8, LANES)).astype(BF16))[:, 0:1]
    start = member * starts
    slot_row = jnp.sum(place + TILE * start, axis=0, keepdims=True)
    same = jnp.where(iota((256, 256), 0) == iota((256, 256), 1), 1.0, 0.0).astype(BF16)
    slot_column = jnp.sum(
        dot_nt(same, place.astype(BF16)) + TILE * dot_nt(same, start.astype(BF16)),
        axis=1,
        keepdims=True,
    )
    unpick[...] = jnp.where(
        slot_column == iota((256, PAD_SLOTS), 1).astype(F32), 1.0, 0.0
    ).astype(BF16)
    pick[...] = jnp.where(
        slot_row == iota((SLOTS, 256), 0).astype(F32), 1.0, 0.0
    ).astype(BF16)
    answers[SLOTS:, :] = jnp.zeros((PAD_SLOTS - SLOTS, LANES), BF16)
    tile_regimes = [0] * TILES
    used = 0
    for r in range(REGIMES - 1):
        named = jnp.sum(jnp.where(regimes == r, 1, 0))
        used = used + (named + (TILE - 1)) // TILE
        tile_regimes = [number + jnp.where(t >= used, 1, 0) for t, number in enumerate(tile_regimes)]

    level_of = iota((TILE, LANES), 1) % LEVELS
    square = jnp.zeros((LANES, LANES), BF16)

    def beside(a, b):
        return jnp.concatenate([a, b], axis=1)

    def over(a, b):
        return jnp.concatenate([a, b], axis=0)

    zero = jnp.zeros((TILE, LANES), BF16)

    def in_pairs(levels):
        return jnp.concatenate([beside(levels[m], levels[m + 1]) for m in range(0, LEVELS, 2)], axis=0)

    def out_of_pairs(rows):
        return [
            rows[m // 2 * TILE : (m // 2 + 1) * TILE, m % 2 * LANES : (m % 2 + 1) * LANES]
            for m in range(LEVELS)
        ]

    def both(tap):
        return over(beside(tap, square), beside(square, tap))

    def lifted(t):
        columns = ordered[t * TILE : (t + 1) * TILE, :]
        masked = [jnp.where(level_of == m, columns, zero) for m in range(LEVELS)]
        return out_of_pairs(dot(in_pairs(masked), both(lift_map[tile_regimes[t]])))

    def layered(t, layer, halves):
        spacing = 2**layer
        below, centre, above = (conv[layer][tile_regimes[t], i] for i in range(3))
        active = []
        for half in halves:
            u = half.astype(BF16)
            active.append(u + u * jnp.tanh(u))
        low = [m for m in range(LEVELS) if m // spacing % 2 == 0]
        pieces = [[active[m] for m in low], [active[m + spacing] for m in low]]
        taps = over(beside(centre, above), beside(below, centre))
        if 2 * spacing < LEVELS:
            pieces.append([active[m - spacing] if m >= spacing else zero for m in low])
            pieces.append(
                [active[m + 2 * spacing] if m + 2 * spacing < LEVELS else zero for m in low]
            )
            taps = beside(taps, over(beside(below, square), beside(square, above)))
        result = dot_nt(
            jnp.concatenate([jnp.concatenate(piece, axis=0) for piece in pieces], axis=1), taps
        )
        halves = list(halves)
        for p, m in enumerate(low):
            rows = slice(p * TILE, (p + 1) * TILE)
            halves[m] = halves[m] + result[rows, :LANES]
            halves[m + spacing] = halves[m + spacing] + result[rows, LANES:]
        return halves

    def answered(t, halves):
        rows = in_pairs([half.astype(BF16) for half in halves])
        pieces = out_of_pairs(dot_nt(rows, both(out_map[tile_regimes[t]])))
        answer = jnp.zeros((TILE, LANES), F32)
        for m in range(LEVELS):
            answer = jnp.where(level_of == m, pieces[m], answer)
        return answer.astype(BF16)

    def network(first_time):
        tiles = [lifted(t) for t in range(TILES)]
        for layer in range(LAYERS):
            if first_time:
                for j in range(3):
                    weights[j][1 + layer].wait_recv()
            tiles = [layered(t, layer, tiles[t]) for t in range(TILES)]
        results = [answered(t, tiles[t]) for t in range(TILES)]
        for t in range(TILES):
            answers[t * TILE : (t + 1) * TILE, :] = results[t]

    def advance(x_from, rows, safe):
        more = 2 * (4 if safe else 0)
        ys = slice(Y0 - 4, Y0 + SIDE + 4)
        at = X0 - 4 + x_from if safe else X0 - 4 + (SAFE + 8) * upper
        xs = pl.ds(at, rows + more)
        first[xs, ys, :] = field[xs, ys, :] + (1.0 / 6.0) * local_tendency(
            field, east, north, flux, at, rows + more, ys
        )
        more = 2 * (2 if safe else 0)
        ys = slice(Y0 - 2, Y0 + SIDE + 2)
        at = X0 - 2 + x_from if safe else X0 - 2 + (SAFE + 4) * upper
        xs = pl.ds(at, rows + more)
        second[xs, ys, :] = (
            0.75 * field[xs, ys, :]
            + 0.25 * first[xs, ys, :]
            + (0.25 / 6.0) * local_tendency(first, east, north, flux, at, rows + more, ys)
        )
        ys = slice(Y0, Y0 + SIDE)
        at = X0 + x_from
        xs = pl.ds(at, rows)
        value = (
            (1.0 / 3.0) * field[xs, ys, :]
            + (2.0 / 3.0) * second[xs, ys, :]
            + (1.0 / 9.0) * local_tendency(second, east, north, flux, at, rows, ys)
        )
        cells = pl.ds(pl.multiple_of(x_from * SIDE, SIDE), rows * SIDE)
        dyn[cells, :] = value.reshape(rows * SIDE, LANES)

    for step in range(STEPS):
        if step:
            pack(step)
            halo = [halo_copy(step, k) for k in range(8)]
            for copy in halo:
                copy.start()
        receive_y(step)
        receive_x(step, 1 - upper)
        advance(safe_from, SAFE, True)
        if step == 0:
            for j in range(3):
                weights[j][0].wait_recv()
            row, column = iota((LANES, 16), 0), iota((LANES, 16), 1)
            to_lift = jnp.where(row // LEVELS == column, 0.5, 0.0).astype(BF16)
            to_out = jnp.where(row // LEVELS + VARS == column, 2.0, 0.0).astype(BF16)
            for r in range(REGIMES):
                lift_map[r] = dot(to_lift, small[r]).astype(BF16)
                out_map[r] = dot(to_out, small[r]).astype(BF16)
        receive_x(step, upper)
        advance(late_from, LATE, False)
        ordered[...] = dot(pick[...], dyn[...].astype(BF16)).astype(BF16)
        network(step == 0)
        final = dyn[...] + dot(unpick[...], answers[...])
        if step < STEPS - 1:
            field[X0 : X0 + SIDE, Y0 : Y0 + SIDE, :] = final.reshape(SIDE, SIDE, LANES)
        else:
            out_ref[...] = final
        for copy in halo:
            copy.wait_send()
    for j in range(3):
        for copy in weights[j]:
            copy.wait_send()


def per_device(state, winds, regime_table, emu_lift, emu_conv, emu_output):
    cells = SIDE * SIDE
    padded = pltpu.VMEM((PAD_X, PAD_Y, LANES), F32)
    dma = pltpu.SemaphoreType.DMA
    result = pl.pallas_call(
        kernel,
        out_shape=jax.ShapeDtypeStruct((cells, LANES), F32),
        in_specs=[pl.BlockSpec(memory_space=pltpu.HBM)] * 6,
        out_specs=pl.BlockSpec(memory_space=pltpu.VMEM),
        scratch_shapes=[
            pltpu.VMEM((LANES * SIDE, SIDE), F32),
            pltpu.VMEM((2 * LEVELS * SIDE, SIDE), F32),
            pltpu.VMEM((1, cells), jnp.int32),
            pltpu.VMEM((VARS, LANES), BF16),
            pltpu.VMEM((VARS, LANES), BF16),
            pltpu.VMEM((3 * LAYERS, LANES, LANES), BF16),
            padded, padded, padded, padded, padded,
            pltpu.VMEM((24, PAD_Y, LANES), F32),
            pltpu.VMEM((4, CORNER * CORNER, LANES), F32),
            pltpu.VMEM((STEPS, 2, 128, LANES), BF16),
            pltpu.VMEM((STEPS, 2, 128, LANES), BF16),
            pltpu.VMEM((STEPS, 2, 160, LANES), BF16),
            pltpu.VMEM((STEPS, 2, 160, LANES), BF16),
            pltpu.VMEM((STEPS, 4, 32, LANES), BF16),
            pltpu.VMEM((STEPS, 4, 32, LANES), BF16),
            *[pltpu.VMEM((REGIMES, 3, LANES, LANES), BF16)] * LAYERS,
            pltpu.VMEM((REGIMES, 2 * VARS, LANES), BF16),
            pltpu.VMEM((REGIMES, LANES, LANES), BF16),
            pltpu.VMEM((REGIMES, LANES, LANES), BF16),
            pltpu.VMEM((LANES, 8 * LANES), BF16),
            pltpu.VMEM((SLOTS, cells), BF16),
            pltpu.VMEM((cells, PAD_SLOTS), BF16),
            pltpu.VMEM((SLOTS, LANES), BF16),
            pltpu.VMEM((PAD_SLOTS, LANES), BF16),
            pltpu.VMEM((cells, LANES), F32),
            dma((6,)),
            dma((STEPS, 8)), dma((STEPS, 8)),
            dma((3, LAYERS)), dma((3, LAYERS)),
            dma((3,)), dma((3,)),
        ],
        compiler_params=pltpu.CompilerParams(
            collective_id=0, has_side_effects=True, vmem_limit_bytes=32 * 2**20
        ),
    )(
        *[
            pltpu.with_memory_space_constraint(operand, pltpu.HBM)
            for operand in (
                state.reshape(LANES * SIDE, SIDE),
                winds.reshape(2 * LEVELS * SIDE, SIDE),
                regime_table.reshape(1, cells),
                emu_lift[0].T,
                emu_output[0],
                emu_conv.reshape(3 * LAYERS, LANES, LANES),
            )
        ]
    )
    return result.reshape(SIDE, SIDE, VARS, LEVELS).transpose(2, 3, 0, 1)


def solution(mesh):
    in_specs = (
        P(None, None, "tile", ("sect", "emu")),
        P(None, None, "tile", ("sect", "emu")),
        P("tile", ("sect", "emu"), None, None),
        P("sect", None, None),
        P("sect", None, None, None, None),
        P("sect", None, None),
    )
    out_specs = P(None, None, "tile", ("sect", "emu"))
    return jax.shard_map(
        per_device, mesh=mesh, in_specs=in_specs, out_specs=out_specs, check_vma=False
    )
```

```python
import functools

import jax
import jax.numpy as jnp
from jax import lax
from jax.experimental import pallas as pl
from jax.experimental.pallas import tpu as pltpu
from jax.sharding import PartitionSpec as P

MESH = pl.DeviceIdType.MESH
STEPS = 2
SIDE = 16
LANES = 128
VARS = 8
LEVELS = 16
REGIMES = 4
LAYERS = 4
TILE = 32
LATE = 6
SAFE = SIDE - LATE
TILES = 11
SLOTS = TILES * TILE
PAD_SLOTS = 384
CORNER = 4
X0, Y0 = 8, 8
PAD_X, PAD_Y = 32, 32
DIRECTIONS = ((1, 1), (1, -1), (-1, 1), (-1, -1), (1, 0), (-1, 0), (0, 1), (0, -1))
BF16 = jnp.bfloat16
F32 = jnp.float32


def dot(a, b):
    return jnp.dot(a, b, preferred_element_type=F32)


def dot_nt(a, b):
    return lax.dot_general(a, b, (((1,), (1,)), ((), ())), preferred_element_type=F32)


def iota(shape, dim):
    return lax.broadcasted_iota(jnp.int32, shape, dim)


def field_rows(dx, dy):
    return 96 if dy == 0 else 128 if dx == 0 else CORNER * CORNER


def wind_rows(dx, dy):
    return 16 if dx and dy else 32


def sent_box(dx, dy):
    deep_x, deep_y = (CORNER, CORNER) if dx and dy else (6, 8)
    xs = slice(X0, X0 + deep_x) if dx < 0 else slice(X0 + SIDE - deep_x, X0 + SIDE)
    ys = slice(Y0, Y0 + deep_y) if dy < 0 else slice(Y0 + SIDE - deep_y, Y0 + SIDE)
    return xs if dx else slice(X0, X0 + SIDE), ys if dy else slice(Y0, Y0 + SIDE)


def wind_groups(dx, dy):
    ys = slice(Y0, Y0 + SIDE) if dy == 0 else slice(Y0 + 8, Y0 + 16) if dy > 0 else slice(Y0, Y0 + 8)
    if dx == 0:
        return [(slice(X0 + 4 * g, X0 + 4 * g + 4), ys) for g in range(4)]
    base = X0 + 8 if dx > 0 else X0
    return [(slice(base + 2 * g, base + 2 * g + 2), ys) for g in range(4)]


def local_tendency(src, east, north, flux, x_from, nx, ys):
    ny = ys.stop - ys.start

    def face_flux(speed, before, center, after, beyond):
        both = 2.0 * (center + after)
        up = jnp.maximum(speed, 0.0)
        down = jnp.minimum(speed, 0.0)
        return up * (both + 3.0 * center - before) + down * (both + 3.0 * after - beyond)

    along_x = src[pl.ds(x_from - 2, nx + 4), ys, :]
    flux_x = face_flux(
        east[pl.ds(x_from - 1, nx + 1), ys, :],
        along_x[0 : nx + 1],
        along_x[1 : nx + 2],
        along_x[2 : nx + 3],
        along_x[3 : nx + 4],
    )
    total = flux_x[:nx] - flux_x[1:]
    xs = pl.ds(x_from, nx)
    start, stop = ys.start - 1, ys.stop
    flux[0:nx, 0 : ny + 1, :] = face_flux(
        north[xs, start:stop, :],
        src[xs, start - 1 : stop - 1, :],
        src[xs, start:stop, :],
        src[xs, start + 1 : stop + 1, :],
        src[xs, start + 2 : stop + 2, :],
    )
    return total + (flux[0:nx, 0:ny, :] - flux[0:nx, 1 : ny + 1, :])


def kernel(
    state_ref, wind_ref, regime_ref, lift_ref, output_ref, taps_ref, out_ref,
    state_in, wind_in, regime_in, lift_in, output_in, taps_in,
    field, first, second, east, north, flux, stage,
    send_x, recv_x, send_y, recv_y, send_c, recv_c,
    conv_0, conv_1, conv_2, conv_3, small, lift_map, out_map, spread, pick, unpick, ordered, answers, dyn,
    load_sem, halo_send, halo_recv, weight_send, weight_recv, small_send, small_recv,
):
    count_tile, count_sect, count_emu = (lax.axis_size(n) for n in ("tile", "sect", "emu"))
    tile, sect, emu = (lax.axis_index(n) for n in ("tile", "sect", "emu"))
    along_y = sect * count_emu + emu
    total_y = count_sect * count_emu

    def neighbour(dx, dy):
        y = lax.rem(along_y + (dy + total_y), total_y)
        return (lax.rem(tile + (dx + count_tile), count_tile), y // count_emu, lax.rem(y, count_emu))

    half = count_tile // 2
    upper = lax.rem(tile, half) // (half // 2)
    safe_from, late_from = LATE * (1 - upper), SAFE * upper
    far_tile = lax.rem(tile + half, count_tile)
    core, chip = lax.rem(sect, 2), sect // 2
    partners = (
        (tile, chip * 2 + (1 - core), emu),
        (tile, (1 - chip) * 2 + core, emu),
        (far_tile, (1 - chip) * 2 + core, emu),
    )
    neighbours = [neighbour(dx, dy) for dx, dy in DIRECTIONS]

    conv = (conv_0, conv_1, conv_2, conv_3)
    barrier = pltpu.get_barrier_semaphore()
    for device in (*neighbours, *partners):
        pl.semaphore_signal(barrier, inc=1, device_id=device, device_id_type=MESH)

    loads = [
        pltpu.make_async_copy(src, dst, load_sem.at[i])
        for i, (src, dst) in enumerate(
            (
                (wind_ref, wind_in),
                (state_ref, state_in),
                (taps_ref, taps_in),
                (regime_ref, regime_in),
                (lift_ref, lift_in),
                (output_ref, output_in),
            )
        )
    ]
    for copy in loads:
        copy.start()

    row, column = iota((LANES, 8 * LANES), 0), iota((LANES, 8 * LANES), 1)
    group, part = column // (2 * LANES), (column // LANES) % 2
    chosen = (row // LEVELS == part * 4 + group) & (row % LEVELS == column % LEVELS)
    spread[...] = jnp.where(chosen, 1.0, 0.0).astype(BF16)
    loads[0].wait()
    packed = []
    for j in range(4):
        rows = [
            wind_in[pl.ds(c * LEVELS * SIDE + 4 * g + j, LEVELS, stride=SIDE), :]
            for c in range(2)
            for g in range(4)
        ]
        packed.append(jnp.concatenate(rows, axis=0).T)
    wide = dot(jnp.concatenate(packed, axis=0).astype(BF16), spread[...])
    for g in range(4):
        at = (slice(X0 + 4 * g, X0 + 4 * g + 4), slice(Y0, Y0 + SIDE), slice(None))
        east[at] = wide[:, 256 * g : 256 * g + 128].reshape(4, SIDE, LANES)
        north[at] = wide[:, 256 * g + 128 : 256 * g + 256].reshape(4, SIDE, LANES)
    loads[1].wait()
    for x in range(SIDE):
        field[X0 + x, Y0 : Y0 + SIDE, :] = state_in[pl.ds(x, LANES, stride=SIDE), :].T

    def buffers(step, k):
        dx, dy = DIRECTIONS[k]
        if dy == 0:
            return send_x.at[step, k - 4], recv_x.at[step, k - 4]
        if dx == 0:
            return send_y.at[step, k - 6], recv_y.at[step, k - 6]
        return send_c.at[step, k], recv_c.at[step, k]

    def halo_copy(step, k):
        sent, received = buffers(step, k)
        rows = field_rows(*DIRECTIONS[k]) + (wind_rows(*DIRECTIONS[k]) if step == 0 else 0)
        return pltpu.make_async_remote_copy(
            src_ref=sent.at[0:rows],
            dst_ref=received.at[0:rows],
            send_sem=halo_send.at[step, k],
            recv_sem=halo_recv.at[step, k],
            device_id=neighbours[k],
            device_id_type=MESH,
        )

    def pack(step, then=lambda k: None):
        for k, (dx, dy) in enumerate(DIRECTIONS):
            sent, _ = buffers(step, k)
            xs, ys = sent_box(dx, dy)
            rows = field_rows(dx, dy)
            if dx and dy:
                for i in range(CORNER):
                    stage[k, CORNER * i : CORNER * (i + 1), :] = field[xs.start + i, ys, :]
                sent[0:rows, :] = stage[k].astype(BF16)
            else:
                sent[0:rows, :] = field[xs, ys, :].reshape(rows, LANES).astype(BF16)
            if step == 0:
                more = wind_rows(dx, dy)
                quarter = iota((more, LANES), 1) // LEVELS
                packed = jnp.zeros((more, LANES), F32)
                for c, winds in enumerate((east, north)):
                    for g, (gx, gy) in enumerate(wind_groups(dx, dy)):
                        piece = winds[gx, gy, :].reshape(more, LANES)
                        packed = jnp.where(quarter == c * 4 + g, piece, packed)
                sent[rows : rows + more, :] = packed.astype(BF16)
            then(k)

    def arrive(step, k, ref, rows):
        pltpu.make_async_remote_copy(
            src_ref=ref.at[0:rows],
            dst_ref=ref.at[0:rows],
            send_sem=halo_send.at[step, k],
            recv_sem=halo_recv.at[step, k],
            device_id=neighbours[0],
            device_id_type=MESH,
        ).wait_recv()

    def unpack_winds(packed, x_from, ys):
        wide = dot(packed, spread[...])
        ny = ys.stop - ys.start
        deep = packed.shape[0] // ny
        for g in range(4):
            xs = pl.ds(x_from + deep * g, deep)
            east[xs, ys, :] = wide[:, 256 * g : 256 * g + 128].reshape(deep, ny, LANES)
            north[xs, ys, :] = wide[:, 256 * g + 128 : 256 * g + 256].reshape(deep, ny, LANES)

    def receive_y(step):
        for k, ys in ((6, slice(Y0 - 8, Y0)), (7, slice(Y0 + SIDE, Y0 + SIDE + 8))):
            rows, more = 128, 32 if step == 0 else 0
            ref = recv_y.at[step, k - 6]
            arrive(step, k, ref, rows + more)
            field[X0 : X0 + SIDE, ys, :] = ref[0:rows, :].astype(F32).reshape(SIDE, 8, LANES)
            if step == 0:
                unpack_winds(ref[rows : rows + more, :], X0, ys)

    def receive_x(step, side):
        rows, more = 96, 32 if step == 0 else 0
        ref = recv_x.at[step, side]
        arrive(step, 4 + side, ref, rows + more)
        own_y = slice(Y0, Y0 + SIDE)
        xs = pl.ds(X0 - 6 + (SIDE + 6) * side, 6)
        field[xs, own_y, :] = ref[0:rows, :].astype(F32).reshape(6, SIDE, LANES)
        winds_from = X0 - 8 + (SIDE + 8) * side
        if step == 0:
            unpack_winds(ref[rows : rows + more, :], winds_from, own_y)
        x_from = X0 - CORNER + (SIDE + CORNER) * side
        for j, start, wide_start in ((0, Y0 - CORNER, Y0 - 8), (1, Y0 + SIDE, Y0 + SIDE)):
            rows, more = CORNER * CORNER, 16 if step == 0 else 0
            ref = recv_c.at[step, 2 * side + j]
            arrive(step, 2 * side + j, ref, rows + more)
            stage[j] = ref[0:rows, :].astype(F32)
            for i in range(CORNER):
                field[x_from + i, start : start + CORNER, :] = stage[j, CORNER * i : CORNER * (i + 1), :]
            if step == 0:
                unpack_winds(ref[rows : rows + more, :], winds_from, slice(wide_start, wide_start + 8))

    pack(0)
    pl.semaphore_wait(barrier, len(neighbours) + len(partners))
    halo = [halo_copy(0, k) for k in range(8)]
    for copy in halo:
        copy.start()

    for copy in loads[2:]:
        copy.wait()
    for layer in range(LAYERS):
        conv[layer][sect] = 0.5 * taps_in[3 * layer : 3 * layer + 3]
    small[sect] = jnp.concatenate([lift_in[...], output_in[...]], axis=0)

    other = (1 - chip) * 2 + core

    def taps_copy(j, layer, regime, handed=0):
        return pltpu.make_async_remote_copy(
            src_ref=conv[layer].at[regime],
            dst_ref=conv[layer].at[regime],
            send_sem=weight_send.at[handed, j, layer],
            recv_sem=weight_recv.at[handed, j, layer],
            device_id=partners[j],
            device_id_type=MESH,
        )

    def small_copy(j, regime, handed=0):
        return pltpu.make_async_remote_copy(
            src_ref=small.at[regime],
            dst_ref=small.at[regime],
            send_sem=small_send.at[handed, j],
            recv_sem=small_recv.at[handed, j],
            device_id=partners[j],
            device_id_type=MESH,
        )

    route = (1, 2, 1, 2)
    own_small = [small_copy(0, sect), small_copy(1, sect)]
    own_taps = [taps_copy(route[layer], layer, sect) for layer in range(LAYERS)]
    core_taps = [taps_copy(0, layer, sect) for layer in range(LAYERS)]
    handed_small = [small_copy(0, other, 1)]
    handed_taps = [taps_copy(0, layer, other, 1) for layer in range(LAYERS)]
    for copy in own_small + own_taps + core_taps:
        copy.start()
    outgoing = own_small + own_taps + core_taps + handed_small + handed_taps

    def hand_on(*layers):
        for layer in layers:
            taps_copy(route[layer], layer, other).wait_recv()
            handed_taps[layer].start()

    arriving = [(core_taps[layer], handed_taps[layer]) for layer in range(LAYERS)]

    regimes = regime_in[...]
    member = jnp.where(regimes == iota((8, 256), 0), 1.0, 0.0)
    earlier = jnp.where(iota((256, 256), 0) < iota((256, 256), 1), 1.0, 0.0).astype(BF16)
    place = member * dot(member.astype(BF16), earlier)
    tiles = jnp.floor((jnp.sum(member, axis=1, keepdims=True) + (TILE - 1)) * (1.0 / TILE))
    before = jnp.where(iota((8, 8), 1) < iota((8, 8), 0), 1.0, 0.0).astype(BF16)
    starts = dot(before, jnp.broadcast_to(tiles, (8, LANES)).astype(BF16))[:, 0:1]
    start = member * starts
    slot_row = jnp.sum(place + TILE * start, axis=0, keepdims=True)
    same = jnp.where(iota((256, 256), 0) == iota((256, 256), 1), 1.0, 0.0).astype(BF16)
    slot_column = jnp.sum(
        dot_nt(same, place.astype(BF16)) + TILE * dot_nt(same, start.astype(BF16)),
        axis=1,
        keepdims=True,
    )
    unpick[...] = jnp.where(
        slot_column == iota((256, PAD_SLOTS), 1).astype(F32), 1.0, 0.0
    ).astype(BF16)
    pick[...] = jnp.where(
        slot_row == iota((SLOTS, 256), 0).astype(F32), 1.0, 0.0
    ).astype(BF16)
    answers[SLOTS:, :] = jnp.zeros((PAD_SLOTS - SLOTS, LANES), BF16)
    tile_regimes = [0] * TILES
    used = 0
    for r in range(REGIMES - 1):
        named = jnp.sum(jnp.where(regimes == r, 1, 0))
        used = used + (named + (TILE - 1)) // TILE
        tile_regimes = [number + jnp.where(t >= used, 1, 0) for t, number in enumerate(tile_regimes)]

    level_of = iota((TILE, LANES), 1) % LEVELS
    square = jnp.zeros((LANES, LANES), BF16)

    def beside(a, b):
        return jnp.concatenate([a, b], axis=1)

    def over(a, b):
        return jnp.concatenate([a, b], axis=0)

    zero = jnp.zeros((TILE, LANES), BF16)

    def in_pairs(levels):
        return jnp.concatenate([beside(levels[m], levels[m + 1]) for m in range(0, LEVELS, 2)], axis=0)

    def out_of_pairs(rows):
        return [
            rows[m // 2 * TILE : (m // 2 + 1) * TILE, m % 2 * LANES : (m % 2 + 1) * LANES]
            for m in range(LEVELS)
        ]

    def both(tap):
        return over(beside(tap, square), beside(square, tap))

    def lifted(t):
        columns = ordered[t * TILE : (t + 1) * TILE, :]
        masked = [jnp.where(level_of == m, columns, zero) for m in range(LEVELS)]
        return out_of_pairs(dot(in_pairs(masked), both(lift_map[tile_regimes[t]])))

    def layered(t, layer, halves):
        spacing = 2**layer
        below, centre, above = (conv[layer][tile_regimes[t], i] for i in range(3))
        active = []
        for half in halves:
            u = half.astype(BF16)
            active.append(u + u * jnp.tanh(u))
        low = [m for m in range(LEVELS) if m // spacing % 2 == 0]
        pieces = [[active[m] for m in low], [active[m + spacing] for m in low]]
        taps = over(beside(centre, above), beside(below, centre))
        if 2 * spacing < LEVELS:
            pieces.append([active[m - spacing] if m >= spacing else zero for m in low])
            pieces.append(
                [active[m + 2 * spacing] if m + 2 * spacing < LEVELS else zero for m in low]
            )
            taps = beside(taps, over(beside(below, square), beside(square, above)))
        result = dot_nt(
            jnp.concatenate([jnp.concatenate(piece, axis=0) for piece in pieces], axis=1), taps
        )
        halves = list(halves)
        for p, m in enumerate(low):
            rows = slice(p * TILE, (p + 1) * TILE)
            halves[m] = halves[m] + result[rows, :LANES]
            halves[m + spacing] = halves[m + spacing] + result[rows, LANES:]
        return halves

    def answered(t, halves):
        rows = in_pairs([half.astype(BF16) for half in halves])
        pieces = out_of_pairs(dot_nt(rows, both(out_map[tile_regimes[t]])))
        answer = jnp.zeros((TILE, LANES), F32)
        for m in range(LEVELS):
            answer = jnp.where(level_of == m, pieces[m], answer)
        return answer.astype(BF16)

    def network(first_time):
        tiles = [lifted(t) for t in range(TILES)]
        for layer in range(LAYERS):
            if first_time:
                for copy in arriving[layer]:
                    copy.wait_recv()
            tiles = [layered(t, layer, tiles[t]) for t in range(TILES)]
            if first_time and layer == 0:
                hand_on(2, 3)
        results = [answered(t, tiles[t]) for t in range(TILES)]
        for t in range(TILES):
            answers[t * TILE : (t + 1) * TILE, :] = results[t]

    def advance(x_from, rows, safe):
        more = 2 * (4 if safe else 0)
        ys = slice(Y0 - 4, Y0 + SIDE + 4)
        at = X0 - 4 + x_from if safe else X0 - 4 + (SAFE + 8) * upper
        xs = pl.ds(at, rows + more)
        first[xs, ys, :] = field[xs, ys, :] + (1.0 / 6.0) * local_tendency(
            field, east, north, flux, at, rows + more, ys
        )
        more = 2 * (2 if safe else 0)
        ys = slice(Y0 - 2, Y0 + SIDE + 2)
        at = X0 - 2 + x_from if safe else X0 - 2 + (SAFE + 4) * upper
        xs = pl.ds(at, rows + more)
        second[xs, ys, :] = (
            0.75 * field[xs, ys, :]
            + 0.25 * first[xs, ys, :]
            + (0.25 / 6.0) * local_tendency(first, east, north, flux, at, rows + more, ys)
        )
        ys = slice(Y0, Y0 + SIDE)
        at = X0 + x_from
        xs = pl.ds(at, rows)
        value = (
            (1.0 / 3.0) * field[xs, ys, :]
            + (2.0 / 3.0) * second[xs, ys, :]
            + (1.0 / 9.0) * local_tendency(second, east, north, flux, at, rows, ys)
        )
        cells = pl.ds(pl.multiple_of(x_from * SIDE, SIDE), rows * SIDE)
        dyn[cells, :] = value.reshape(rows * SIDE, LANES)

    for step in range(STEPS):
        if step:
            halo = [halo_copy(step, k) for k in range(8)]
            pack(step, lambda k: halo[k].start())
        receive_y(step)
        if step == 0:
            small_copy(1, other).wait_recv()
            handed_small[0].start()
        receive_x(step, 1 - upper)
        advance(safe_from, SAFE, True)
        if step == 0:
            hand_on(0, 1)
            own_small[0].wait_recv()
            handed_small[0].wait_recv()
            row, column = iota((LANES, 16), 0), iota((LANES, 16), 1)
            to_lift = jnp.where(row // LEVELS == column, 0.5, 0.0).astype(BF16)
            to_out = jnp.where(row // LEVELS + VARS == column, 2.0, 0.0).astype(BF16)
            for r in range(REGIMES):
                lift_map[r] = dot(to_lift, small[r]).astype(BF16)
                out_map[r] = dot(to_out, small[r]).astype(BF16)
        receive_x(step, upper)
        advance(late_from, LATE, False)
        ordered[...] = dot(pick[...], dyn[...].astype(BF16)).astype(BF16)
        network(step == 0)
        final = dyn[...] + dot(unpick[...], answers[...])
        if step < STEPS - 1:
            field[X0 : X0 + SIDE, Y0 : Y0 + SIDE, :] = final.reshape(SIDE, SIDE, LANES)
        else:
            for x in range(SIDE):
                out_ref[pl.ds(x, LANES, stride=SIDE), :] = final[SIDE * x : SIDE * (x + 1)].T
        for copy in halo:
            copy.wait_send()
    for copy in outgoing:
        copy.wait_send()


def per_device(state, winds, regime_table, emu_lift, emu_conv, emu_output):
    cells = SIDE * SIDE
    padded = pltpu.VMEM((PAD_X, PAD_Y, LANES), F32)
    dma = pltpu.SemaphoreType.DMA
    result = pl.pallas_call(
        kernel,
        out_shape=jax.ShapeDtypeStruct((LANES * SIDE, SIDE), F32),
        in_specs=[pl.BlockSpec(memory_space=pltpu.HBM)] * 6,
        out_specs=pl.BlockSpec(memory_space=pltpu.VMEM),
        scratch_shapes=[
            pltpu.VMEM((LANES * SIDE, SIDE), F32),
            pltpu.VMEM((2 * LEVELS * SIDE, SIDE), F32),
            pltpu.VMEM((1, cells), jnp.int32),
            pltpu.VMEM((VARS, LANES), BF16),
            pltpu.VMEM((VARS, LANES), BF16),
            pltpu.VMEM((3 * LAYERS, LANES, LANES), BF16),
            padded, padded, padded, padded, padded,
            pltpu.VMEM((24, PAD_Y, LANES), F32),
            pltpu.VMEM((4, CORNER * CORNER, LANES), F32),
            pltpu.VMEM((STEPS, 2, 128, LANES), BF16),
            pltpu.VMEM((STEPS, 2, 128, LANES), BF16),
            pltpu.VMEM((STEPS, 2, 160, LANES), BF16),
            pltpu.VMEM((STEPS, 2, 160, LANES), BF16),
            pltpu.VMEM((STEPS, 4, 32, LANES), BF16),
            pltpu.VMEM((STEPS, 4, 32, LANES), BF16),
            *[pltpu.VMEM((REGIMES, 3, LANES, LANES), BF16)] * LAYERS,
            pltpu.VMEM((REGIMES, 2 * VARS, LANES), BF16),
            pltpu.VMEM((REGIMES, LANES, LANES), BF16),
            pltpu.VMEM((REGIMES, LANES, LANES), BF16),
            pltpu.VMEM((LANES, 8 * LANES), BF16),
            pltpu.VMEM((SLOTS, cells), BF16),
            pltpu.VMEM((cells, PAD_SLOTS), BF16),
            pltpu.VMEM((SLOTS, LANES), BF16),
            pltpu.VMEM((PAD_SLOTS, LANES), BF16),
            pltpu.VMEM((cells, LANES), F32),
            dma((6,)),
            dma((STEPS, 8)), dma((STEPS, 8)),
            dma((2, 3, LAYERS)), dma((2, 3, LAYERS)),
            dma((2, 3)), dma((2, 3)),
        ],
        compiler_params=pltpu.CompilerParams(
            collective_id=0, has_side_effects=True, vmem_limit_bytes=32 * 2**20
        ),
    )(
        *[
            pltpu.with_memory_space_constraint(operand, pltpu.HBM)
            for operand in (
                state.reshape(LANES * SIDE, SIDE),
                winds.reshape(2 * LEVELS * SIDE, SIDE),
                regime_table.reshape(1, cells),
                emu_lift[0].T,
                emu_output[0],
                emu_conv.reshape(3 * LAYERS, LANES, LANES),
            )
        ]
    )
    return result.reshape(VARS, LEVELS, SIDE, SIDE)


def solution(mesh):
    in_specs = (
        P(None, None, "tile", ("sect", "emu")),
        P(None, None, "tile", ("sect", "emu")),
        P("tile", ("sect", "emu"), None, None),
        P("sect", None, None),
        P("sect", None, None, None, None),
        P("sect", None, None),
    )
    out_specs = P(None, None, "tile", ("sect", "emu"))
    return jax.shard_map(
        per_device, mesh=mesh, in_specs=in_specs, out_specs=out_specs, check_vma=False
    )
```

```python
import functools

import jax
import jax.numpy as jnp
from jax import lax
from jax.experimental import pallas as pl
from jax.experimental.pallas import tpu as pltpu
from jax.sharding import PartitionSpec as P

MESH = pl.DeviceIdType.MESH
STEPS = 2
SIDE = 16
LANES = 128
VARS = 8
LEVELS = 16
REGIMES = 4
LAYERS = 4
TILE = 32
LATE = 6
SAFE = SIDE - LATE
TILES = 11
SLOTS = TILES * TILE
PAD_SLOTS = 384
CORNER = 4
X0, Y0 = 8, 8
PAD_X, PAD_Y = 32, 40
DIRECTIONS = ((1, 1), (1, -1), (-1, 1), (-1, -1), (1, 0), (-1, 0), (0, 1), (0, -1))
BF16 = jnp.bfloat16
F32 = jnp.float32


def dot(a, b):
    return jnp.dot(a, b, preferred_element_type=F32)


def dot_nt(a, b):
    return lax.dot_general(a, b, (((1,), (1,)), ((), ())), preferred_element_type=F32)


def iota(shape, dim):
    return lax.broadcasted_iota(jnp.int32, shape, dim)


def field_rows(dx, dy):
    return 96 if dy == 0 else 128 if dx == 0 else CORNER * CORNER


def wind_rows(dx, dy):
    return 16 if dx and dy else 32


def sent_box(dx, dy):
    deep_x, deep_y = (CORNER, CORNER) if dx and dy else (6, 8)
    xs = slice(X0, X0 + deep_x) if dx < 0 else slice(X0 + SIDE - deep_x, X0 + SIDE)
    ys = slice(Y0, Y0 + deep_y) if dy < 0 else slice(Y0 + SIDE - deep_y, Y0 + SIDE)
    return xs if dx else slice(X0, X0 + SIDE), ys if dy else slice(Y0, Y0 + SIDE)


def wind_groups(dx, dy):
    ys = slice(Y0, Y0 + SIDE) if dy == 0 else slice(Y0 + 8, Y0 + 16) if dy > 0 else slice(Y0, Y0 + 8)
    if dx == 0:
        return [(slice(X0 + 4 * g, X0 + 4 * g + 4), ys) for g in range(4)]
    base = X0 + 8 if dx > 0 else X0
    return [(slice(base + 2 * g, base + 2 * g + 2), ys) for g in range(4)]


def local_tendency(src, east, north, flux, x_from, nx, ys):
    ny = ys.stop - ys.start

    def face_flux(speed, before, center, after, beyond):
        both = 2.0 * (center + after)
        up = jnp.maximum(speed, 0.0)
        down = jnp.minimum(speed, 0.0)
        return up * (both + 3.0 * center - before) + down * (both + 3.0 * after - beyond)

    along_x = src[pl.ds(x_from - 2, nx + 4), ys, :]
    flux_x = face_flux(
        east[pl.ds(x_from - 1, nx + 1), ys, :],
        along_x[0 : nx + 1],
        along_x[1 : nx + 2],
        along_x[2 : nx + 3],
        along_x[3 : nx + 4],
    )
    total = flux_x[:nx] - flux_x[1:]
    xs = pl.ds(x_from, nx)
    start, stop = ys.start - 1, ys.stop
    flux[0:nx, 0 : ny + 1, :] = face_flux(
        north[xs, start:stop, :],
        src[xs, start - 1 : stop - 1, :],
        src[xs, start:stop, :],
        src[xs, start + 1 : stop + 1, :],
        src[xs, start + 2 : stop + 2, :],
    )
    return total + (flux[0:nx, 0:ny, :] - flux[0:nx, 1 : ny + 1, :])


def kernel(
    state_ref, wind_ref, regime_ref, lift_ref, output_ref, taps_ref, out_ref,
    state_in, wind_in, regime_in, lift_in, output_in, taps_in,
    field, first, second, east, north, flux, stage,
    send_x, recv_x, send_y, recv_y, send_c, recv_c,
    conv_0, conv_1, conv_2, conv_3, small, lift_map, out_map, spread, pick, unpick, ordered, answers, dyn,
    load_sem, halo_send, halo_recv, weight_send, weight_recv, small_send, small_recv,
):
    count_tile, count_sect, count_emu = (lax.axis_size(n) for n in ("tile", "sect", "emu"))
    tile, sect, emu = (lax.axis_index(n) for n in ("tile", "sect", "emu"))
    along_y = sect * count_emu + emu
    total_y = count_sect * count_emu

    def neighbour(dx, dy):
        y = lax.rem(along_y + (dy + total_y), total_y)
        return (lax.rem(tile + (dx + count_tile), count_tile), y // count_emu, lax.rem(y, count_emu))

    half = count_tile // 2
    upper = lax.rem(tile, half) // (half // 2)
    safe_from, late_from = LATE * (1 - upper), SAFE * upper
    far_tile = lax.rem(tile + half, count_tile)
    core, chip = lax.rem(sect, 2), sect // 2
    partners = (
        (tile, chip * 2 + (1 - core), emu),
        (tile, (1 - chip) * 2 + core, emu),
        (far_tile, (1 - chip) * 2 + core, emu),
    )
    neighbours = [neighbour(dx, dy) for dx, dy in DIRECTIONS]

    conv = (conv_0, conv_1, conv_2, conv_3)
    barrier = pltpu.get_barrier_semaphore()
    for device in (*neighbours, *partners):
        pl.semaphore_signal(barrier, inc=1, device_id=device, device_id_type=MESH)

    loads = [
        pltpu.make_async_copy(src, dst, load_sem.at[i])
        for i, (src, dst) in enumerate(
            (
                (wind_ref, wind_in),
                (state_ref, state_in),
                (taps_ref, taps_in),
                (regime_ref, regime_in),
                (lift_ref, lift_in),
                (output_ref, output_in),
            )
        )
    ]
    for copy in loads:
        copy.start()

    row, column = iota((LANES, 8 * LANES), 0), iota((LANES, 8 * LANES), 1)
    group, part = column // (2 * LANES), (column // LANES) % 2
    chosen = (row // LEVELS == part * 4 + group) & (row % LEVELS == column % LEVELS)
    spread[...] = jnp.where(chosen, 1.0, 0.0).astype(BF16)
    loads[0].wait()
    packed = []
    for j in range(4):
        rows = [
            wind_in[pl.ds(c * LEVELS * SIDE + 4 * g + j, LEVELS, stride=SIDE), :]
            for c in range(2)
            for g in range(4)
        ]
        packed.append(jnp.concatenate(rows, axis=0).T)
    wide = dot(jnp.concatenate(packed, axis=0).astype(BF16), spread[...])
    for g in range(4):
        at = (slice(X0 + 4 * g, X0 + 4 * g + 4), slice(Y0, Y0 + SIDE), slice(None))
        east[at] = wide[:, 256 * g : 256 * g + 128].reshape(4, SIDE, LANES)
        north[at] = wide[:, 256 * g + 128 : 256 * g + 256].reshape(4, SIDE, LANES)
    loads[1].wait()
    for x in range(SIDE):
        field[X0 + x, Y0 : Y0 + SIDE, :] = state_in[pl.ds(x, LANES, stride=SIDE), :].T

    def buffers(step, k):
        dx, dy = DIRECTIONS[k]
        if dy == 0:
            return send_x.at[step, k - 4], recv_x.at[step, k - 4]
        if dx == 0:
            return send_y.at[step, k - 6], recv_y.at[step, k - 6]
        return send_c.at[step, k], recv_c.at[step, k]

    def halo_copy(step, k):
        sent, received = buffers(step, k)
        rows = field_rows(*DIRECTIONS[k]) + (wind_rows(*DIRECTIONS[k]) if step == 0 else 0)
        return pltpu.make_async_remote_copy(
            src_ref=sent.at[0:rows],
            dst_ref=received.at[0:rows],
            send_sem=halo_send.at[step, k],
            recv_sem=halo_recv.at[step, k],
            device_id=neighbours[k],
            device_id_type=MESH,
        )

    def pack(step, then=lambda k: None):
        for k, (dx, dy) in enumerate(DIRECTIONS):
            sent, _ = buffers(step, k)
            xs, ys = sent_box(dx, dy)
            rows = field_rows(dx, dy)
            if dx and dy:
                for i in range(CORNER):
                    stage[k, CORNER * i : CORNER * (i + 1), :] = field[xs.start + i, ys, :]
                sent[0:rows, :] = stage[k, 0:rows, :].astype(BF16)
            else:
                sent[0:rows, :] = field[xs, ys, :].reshape(rows, LANES).astype(BF16)
            if step == 0:
                more = wind_rows(dx, dy)
                quarter = iota((more, LANES), 1) // LEVELS
                packed = jnp.zeros((more, LANES), F32)
                for c, winds in enumerate((east, north)):
                    for g, (gx, gy) in enumerate(wind_groups(dx, dy)):
                        piece = winds[gx, gy, :].reshape(more, LANES)
                        packed = jnp.where(quarter == c * 4 + g, piece, packed)
                sent[rows : rows + more, :] = packed.astype(BF16)
            then(k)

    def arrive(step, k, ref, rows):
        pltpu.make_async_remote_copy(
            src_ref=ref.at[0:rows],
            dst_ref=ref.at[0:rows],
            send_sem=halo_send.at[step, k],
            recv_sem=halo_recv.at[step, k],
            device_id=neighbours[0],
            device_id_type=MESH,
        ).wait_recv()

    def unpack_winds(packed, x_from, ys):
        wide = dot(packed, spread[...])
        ny = ys.stop - ys.start
        deep = packed.shape[0] // ny
        for g in range(4):
            xs = pl.ds(x_from + deep * g, deep)
            east[xs, ys, :] = wide[:, 256 * g : 256 * g + 128].reshape(deep, ny, LANES)
            north[xs, ys, :] = wide[:, 256 * g + 128 : 256 * g + 256].reshape(deep, ny, LANES)

    def receive_y(step):
        for k, ys in ((6, slice(Y0 - 8, Y0)), (7, slice(Y0 + SIDE, Y0 + SIDE + 8))):
            rows, more = 128, 32 if step == 0 else 0
            ref = recv_y.at[step, k - 6]
            arrive(step, k, ref, rows + more)
            field[X0 : X0 + SIDE, ys, :] = ref[0:rows, :].astype(F32).reshape(SIDE, 8, LANES)
            if step == 0:
                unpack_winds(ref[rows : rows + more, :], X0, ys)

    def receive_x(step, side):
        rows, more = 96, 32 if step == 0 else 0
        ref = recv_x.at[step, side]
        arrive(step, 4 + side, ref, rows + more)
        own_y = slice(Y0, Y0 + SIDE)
        xs = pl.ds(X0 - 6 + (SIDE + 6) * side, 6)
        field[xs, own_y, :] = ref[0:rows, :].astype(F32).reshape(6, SIDE, LANES)
        winds_from = X0 - 8 + (SIDE + 8) * side
        if step == 0:
            unpack_winds(ref[rows : rows + more, :], winds_from, own_y)
        x_from = X0 - CORNER + (SIDE + CORNER) * side
        for j, start, wide_start in ((0, Y0 - CORNER, Y0 - 8), (1, Y0 + SIDE, Y0 + SIDE)):
            rows, more = CORNER * CORNER, 16 if step == 0 else 0
            ref = recv_c.at[step, 2 * side + j]
            arrive(step, 2 * side + j, ref, rows + more)
            stage[j, 0:rows, :] = ref[0:rows, :].astype(F32)
            for i in range(CORNER):
                field[x_from + i, start : start + CORNER, :] = stage[j, CORNER * i : CORNER * (i + 1), :]
            if step == 0:
                unpack_winds(ref[rows : rows + more, :], winds_from, slice(wide_start, wide_start + 8))

    pack(0)
    pl.semaphore_wait(barrier, len(neighbours) + len(partners))
    halo = [halo_copy(0, k) for k in range(8)]
    for copy in halo:
        copy.start()

    for copy in loads[2:]:
        copy.wait()
    for layer in range(LAYERS):
        conv[layer][sect] = 0.5 * taps_in[3 * layer : 3 * layer + 3]
    small[sect] = jnp.concatenate([lift_in[...], output_in[...]], axis=0)

    other = (1 - chip) * 2 + core

    def taps_copy(j, layer, regime, handed=0):
        return pltpu.make_async_remote_copy(
            src_ref=conv[layer].at[regime],
            dst_ref=conv[layer].at[regime],
            send_sem=weight_send.at[handed, j, layer],
            recv_sem=weight_recv.at[handed, j, layer],
            device_id=partners[j],
            device_id_type=MESH,
        )

    def small_copy(j, regime, handed=0):
        return pltpu.make_async_remote_copy(
            src_ref=small.at[regime],
            dst_ref=small.at[regime],
            send_sem=small_send.at[handed, j],
            recv_sem=small_recv.at[handed, j],
            device_id=partners[j],
            device_id_type=MESH,
        )

    route = (1, 2, 1, 2)
    own_small = [small_copy(0, sect), small_copy(1, sect)]
    own_taps = [taps_copy(route[layer], layer, sect) for layer in range(LAYERS)]
    core_taps = [taps_copy(0, layer, sect) for layer in range(LAYERS)]
    handed_small = [small_copy(0, other, 1)]
    handed_taps = [taps_copy(0, layer, other, 1) for layer in range(LAYERS)]
    for copy in own_small + own_taps + core_taps:
        copy.start()
    outgoing = own_small + own_taps + core_taps + handed_small + handed_taps

    def hand_on(*layers):
        for layer in layers:
            taps_copy(route[layer], layer, other).wait_recv()
            handed_taps[layer].start()

    arriving = [(core_taps[layer], handed_taps[layer]) for layer in range(LAYERS)]

    regimes = regime_in[...]
    member = jnp.where(regimes == iota((8, 256), 0), 1.0, 0.0)
    earlier = jnp.where(iota((256, 256), 0) < iota((256, 256), 1), 1.0, 0.0).astype(BF16)
    place = member * dot(member.astype(BF16), earlier)
    tiles = jnp.floor((jnp.sum(member, axis=1, keepdims=True) + (TILE - 1)) * (1.0 / TILE))
    before = jnp.where(iota((8, 8), 1) < iota((8, 8), 0), 1.0, 0.0).astype(BF16)
    starts = dot(before, jnp.broadcast_to(tiles, (8, LANES)).astype(BF16))[:, 0:1]
    start = member * starts
    slot_row = jnp.sum(place + TILE * start, axis=0, keepdims=True)
    same = jnp.where(iota((256, 256), 0) == iota((256, 256), 1), 1.0, 0.0).astype(BF16)
    slot_column = jnp.sum(
        dot_nt(same, place.astype(BF16)) + TILE * dot_nt(same, start.astype(BF16)),
        axis=1,
        keepdims=True,
    )
    unpick[...] = jnp.where(
        slot_column == iota((256, PAD_SLOTS), 1).astype(F32), 1.0, 0.0
    ).astype(BF16)
    pick[...] = jnp.where(
        slot_row == iota((SLOTS, 256), 0).astype(F32), 1.0, 0.0
    ).astype(BF16)
    answers[SLOTS:, :] = jnp.zeros((PAD_SLOTS - SLOTS, LANES), BF16)
    tile_regimes = [0] * TILES
    used = 0
    for r in range(REGIMES - 1):
        named = jnp.sum(jnp.where(regimes == r, 1, 0))
        used = used + (named + (TILE - 1)) // TILE
        tile_regimes = [number + jnp.where(t >= used, 1, 0) for t, number in enumerate(tile_regimes)]

    level_of = iota((TILE, LANES), 1) % LEVELS
    square = jnp.zeros((LANES, LANES), BF16)

    def beside(a, b):
        return jnp.concatenate([a, b], axis=1)

    def over(a, b):
        return jnp.concatenate([a, b], axis=0)

    zero = jnp.zeros((TILE, LANES), BF16)

    def in_pairs(levels):
        return jnp.concatenate([beside(levels[m], levels[m + 1]) for m in range(0, LEVELS, 2)], axis=0)

    def out_of_pairs(rows):
        return [
            rows[m // 2 * TILE : (m // 2 + 1) * TILE, m % 2 * LANES : (m % 2 + 1) * LANES]
            for m in range(LEVELS)
        ]

    def both(tap):
        return over(beside(tap, square), beside(square, tap))

    def lifted(t):
        columns = ordered[t * TILE : (t + 1) * TILE, :]
        masked = [jnp.where(level_of == m, columns, zero) for m in range(LEVELS)]
        return out_of_pairs(dot(in_pairs(masked), both(lift_map[tile_regimes[t]])))

    def layered(t, layer, halves):
        spacing = 2**layer
        below, centre, above = (conv[layer][tile_regimes[t], i] for i in range(3))
        active = []
        for half in halves:
            u = half.astype(BF16)
            active.append(u + u * jnp.tanh(u))
        low = [m for m in range(LEVELS) if m // spacing % 2 == 0]
        pieces = [[active[m] for m in low], [active[m + spacing] for m in low]]
        taps = over(beside(centre, above), beside(below, centre))
        if 2 * spacing < LEVELS:
            pieces.append([active[m - spacing] if m >= spacing else zero for m in low])
            pieces.append(
                [active[m + 2 * spacing] if m + 2 * spacing < LEVELS else zero for m in low]
            )
            taps = beside(taps, over(beside(below, square), beside(square, above)))
        result = dot_nt(
            jnp.concatenate([jnp.concatenate(piece, axis=0) for piece in pieces], axis=1), taps
        )
        halves = list(halves)
        for p, m in enumerate(low):
            rows = slice(p * TILE, (p + 1) * TILE)
            halves[m] = halves[m] + result[rows, :LANES]
            halves[m + spacing] = halves[m + spacing] + result[rows, LANES:]
        return halves

    def answered(t, halves):
        rows = in_pairs([half.astype(BF16) for half in halves])
        pieces = out_of_pairs(dot_nt(rows, both(out_map[tile_regimes[t]])))
        answer = jnp.zeros((TILE, LANES), F32)
        for m in range(LEVELS):
            answer = jnp.where(level_of == m, pieces[m], answer)
        return answer.astype(BF16)

    def network(first_time):
        tiles = [lifted(t) for t in range(TILES)]
        for layer in range(LAYERS):
            if first_time:
                for copy in arriving[layer]:
                    copy.wait_recv()
            tiles = [layered(t, layer, tiles[t]) for t in range(TILES)]
            if first_time and layer == 0:
                hand_on(2, 3)
        results = [answered(t, tiles[t]) for t in range(TILES)]
        for t in range(TILES):
            answers[t * TILE : (t + 1) * TILE, :] = results[t]

    def advance(x_from, rows, safe):
        more = 2 * (4 if safe else 0)
        ys = slice(Y0 - 4, Y0 + SIDE + 4)
        at = X0 - 4 + x_from if safe else X0 - 4 + (SAFE + 8) * upper
        xs = pl.ds(at, rows + more)
        first[xs, ys, :] = field[xs, ys, :] + (1.0 / 6.0) * local_tendency(
            field, east, north, flux, at, rows + more, ys
        )
        more = 2 * (2 if safe else 0)
        ys = slice(Y0 - 2, Y0 + SIDE + 2)
        at = X0 - 2 + x_from if safe else X0 - 2 + (SAFE + 4) * upper
        xs = pl.ds(at, rows + more)
        second[xs, ys, :] = (
            0.75 * field[xs, ys, :]
            + 0.25 * first[xs, ys, :]
            + (0.25 / 6.0) * local_tendency(first, east, north, flux, at, rows + more, ys)
        )
        ys = slice(Y0, Y0 + SIDE)
        at = X0 + x_from
        xs = pl.ds(at, rows)
        value = (
            (1.0 / 3.0) * field[xs, ys, :]
            + (2.0 / 3.0) * second[xs, ys, :]
            + (1.0 / 9.0) * local_tendency(second, east, north, flux, at, rows, ys)
        )
        cells = pl.ds(pl.multiple_of(x_from * SIDE, SIDE), rows * SIDE)
        dyn[cells, :] = value.reshape(rows * SIDE, LANES)

    for step in range(STEPS):
        if step:
            halo = [halo_copy(step, k) for k in range(8)]
            pack(step, lambda k: halo[k].start())
        receive_y(step)
        if step == 0:
            small_copy(1, other).wait_recv()
            handed_small[0].start()
        receive_x(step, 1 - upper)
        advance(safe_from, SAFE, True)
        if step == 0:
            hand_on(0, 1)
            own_small[0].wait_recv()
            handed_small[0].wait_recv()
            row, column = iota((LANES, 16), 0), iota((LANES, 16), 1)
            to_lift = jnp.where(row // LEVELS == column, 0.5, 0.0).astype(BF16)
            to_out = jnp.where(row // LEVELS + VARS == column, 2.0, 0.0).astype(BF16)
            for r in range(REGIMES):
                lift_map[r] = dot(to_lift, small[r]).astype(BF16)
                out_map[r] = dot(to_out, small[r]).astype(BF16)
        receive_x(step, upper)
        advance(late_from, LATE, False)
        ordered[...] = dot(pick[...], dyn[...].astype(BF16)).astype(BF16)
        network(step == 0)
        final = dyn[...] + dot(unpick[...], answers[...])
        if step < STEPS - 1:
            field[X0 : X0 + SIDE, Y0 : Y0 + SIDE, :] = final.reshape(SIDE, SIDE, LANES)
        else:
            for x in range(SIDE):
                out_ref[pl.ds(x, LANES, stride=SIDE), :] = final[SIDE * x : SIDE * (x + 1)].T
        for copy in halo:
            copy.wait_send()
    for copy in outgoing:
        copy.wait_send()


def per_device(state, winds, regime_table, emu_lift, emu_conv, emu_output):
    cells = SIDE * SIDE
    padded = pltpu.VMEM((PAD_X, PAD_Y, LANES), F32)
    dma = pltpu.SemaphoreType.DMA
    result = pl.pallas_call(
        kernel,
        out_shape=jax.ShapeDtypeStruct((LANES * SIDE, SIDE), F32),
        in_specs=[pl.BlockSpec(memory_space=pltpu.HBM)] * 6,
        out_specs=pl.BlockSpec(memory_space=pltpu.VMEM),
        scratch_shapes=[
            pltpu.VMEM((LANES * SIDE, SIDE), F32),
            pltpu.VMEM((2 * LEVELS * SIDE, SIDE), F32),
            pltpu.VMEM((1, cells), jnp.int32),
            pltpu.VMEM((VARS, LANES), BF16),
            pltpu.VMEM((VARS, LANES), BF16),
            pltpu.VMEM((3 * LAYERS, LANES, LANES), BF16),
            padded, padded, padded, padded, padded,
            pltpu.VMEM((24, PAD_Y, LANES), F32),
            pltpu.VMEM((4, CORNER * CORNER + 8, LANES), F32),
            pltpu.VMEM((STEPS, 2, 128, LANES), BF16),
            pltpu.VMEM((STEPS, 2, 128, LANES), BF16),
            pltpu.VMEM((STEPS, 2, 160, LANES), BF16),
            pltpu.VMEM((STEPS, 2, 160, LANES), BF16),
            pltpu.VMEM((STEPS, 4, 32, LANES), BF16),
            pltpu.VMEM((STEPS, 4, 32, LANES), BF16),
            *[pltpu.VMEM((REGIMES, 3, LANES, LANES), BF16)] * LAYERS,
            pltpu.VMEM((REGIMES, 2 * VARS, LANES), BF16),
            pltpu.VMEM((REGIMES, LANES, LANES), BF16),
            pltpu.VMEM((REGIMES, LANES, LANES), BF16),
            pltpu.VMEM((LANES, 8 * LANES), BF16),
            pltpu.VMEM((SLOTS, cells), BF16),
            pltpu.VMEM((cells, PAD_SLOTS), BF16),
            pltpu.VMEM((SLOTS, LANES), BF16),
            pltpu.VMEM((PAD_SLOTS, LANES), BF16),
            pltpu.VMEM((cells, LANES), F32),
            dma((6,)),
            dma((STEPS, 8)), dma((STEPS, 8)),
            dma((2, 3, LAYERS)), dma((2, 3, LAYERS)),
            dma((2, 3)), dma((2, 3)),
        ],
        compiler_params=pltpu.CompilerParams(
            collective_id=0, has_side_effects=True, vmem_limit_bytes=32 * 2**20
        ),
    )(
        *[
            pltpu.with_memory_space_constraint(operand, pltpu.HBM)
            for operand in (
                state.reshape(LANES * SIDE, SIDE),
                winds.reshape(2 * LEVELS * SIDE, SIDE),
                regime_table.reshape(1, cells),
                emu_lift[0].T,
                emu_output[0],
                emu_conv.reshape(3 * LAYERS, LANES, LANES),
            )
        ]
    )
    return result.reshape(VARS, LEVELS, SIDE, SIDE)


def solution(mesh):
    in_specs = (
        P(None, None, "tile", ("sect", "emu")),
        P(None, None, "tile", ("sect", "emu")),
        P("tile", ("sect", "emu"), None, None),
        P("sect", None, None),
        P("sect", None, None, None, None),
        P("sect", None, None),
    )
    out_specs = P(None, None, "tile", ("sect", "emu"))
    return jax.shard_map(
        per_device, mesh=mesh, in_specs=in_specs, out_specs=out_specs, check_vma=False
    )
```
